256 devices in a mesh: grp: 16 (over z, core), inner: 16 (over y, x).
Axes of the slice: x: 4, y: 4, z: 8, core: 2. Of those that a mesh axis runs over, the one named last changes fastest.
Arguments:
- snapshots: float32 [64, 2097152], P(None, ('grp', 'inner')), as said below
Outputs:
- basis: float32 [64, 2097152], P(None, ('grp', 'inner'))
- triangle: float32 [64, 64], replicated
Inputs may be any that keep to these rules, and one draw needn't show every extreme that they name: The rows of snapshots are linearly independent.
All inputs are finite; a program needn't handle non-finite values.
Results may differ from the reference program's by a relative error of at most 0.0003.
Values sent between devices are 32-bit elements; how exact they have to be, the bound alone decides.
A program may use at most 64 MiB of HBM per device.

```python
import math
import jax
import jax.numpy as jnp
from jax import lax

K = 64
ROWS_DEV = 8192
ROWS = 2097152
N_GRP = 16
N_INNER = 16


def draw_snapshots(key, part):
    key = jax.random.fold_in(key, 7)
    keys = jax.random.split(key, 6)
    region = jnp.exp(jnp.log(10.0) * jax.random.uniform(keys[1], (1, ROWS // (ROWS_DEV // 4)), jnp.float32))
    region = jnp.repeat(region, ROWS_DEV // 4, axis=1)
    cells = jnp.exp(jnp.log(3.0) * jax.random.uniform(keys[2], (1, ROWS), jnp.float32))
    spread = jnp.log(2.5)
    base = jax.random.normal(keys[0], (K, ROWS), jnp.float32)
    shared = jax.random.normal(keys[4], (1, ROWS), jnp.float32)
    columns = jnp.exp(spread * jax.random.uniform(keys[3], (K, 1), jnp.float32))
    weights = 0.01 * jnp.exp(jnp.log(3.0) * jax.random.uniform(keys[5], (K, 1), jnp.float32))
    return ((shared + weights * base) * region * cells * columns).astype(jnp.float32)


def setup_inputs(seed: int = 0) -> dict:
    key_list = jax.random.split(jax.random.key(seed), 2)
    return {
        "snapshots": draw_snapshots(jax.random.fold_in(key_list[1], 71), 0),
    }


def gram_of(rows):
    count = rows.shape[0]
    blocks_count = N_GRP * N_INNER
    blocks = rows.reshape(count, blocks_count, ROWS // blocks_count)
    partial_sums = jnp.einsum('kbn,jbn->bkj', blocks.astype(jnp.float32), blocks.astype(jnp.float32), precision=lax.Precision.HIGHEST, preferred_element_type=jnp.float32)
    for level in range(blocks_count.bit_length() - 1):
        partial_sums = partial_sums[0::2] + partial_sums[1::2]
    return partial_sums[0]

def reference(snapshots):
    low_first = jnp.linalg.cholesky(gram_of(snapshots))
    first = jax.scipy.linalg.solve_triangular(low_first, snapshots, lower=True)
    low_second = jnp.linalg.cholesky(gram_of(first))
    second = jax.scipy.linalg.solve_triangular(low_second, first, lower=True)
    upper = jnp.dot(low_first, low_second, precision=lax.Precision.HIGHEST).T
    root = math.sqrt(ROWS)
    return (second * root, upper / root)
```

```python
import functools
import math

import jax
import jax.numpy as jnp
from jax import lax
from jax.experimental import pallas as pl
from jax.experimental.pallas import tpu as pltpu
from jax.sharding import PartitionSpec as P

F32 = jnp.float32
BF16 = jnp.bfloat16
EXACT = lax.Precision.HIGHEST
NT = (((1,), (1,)), ((), ()))
NN = (((1,), (0,)), ((), ()))


def two_sum(a, b):
    s = a + b
    t = s - a
    return s, (a - (s - t)) + (b - t)


def quick_two_sum(a, b):
    s = a + b
    return s, b - (s - a)


def power_above(m):
    c = m * 8388609.0
    return 2.0 * (c - (c - m))


def cut(x, scale, exponents):
    pieces = []
    for e in exponents:
        magic = scale * (1.5 * 2.0 ** (23 + e))
        piece = (x + magic) - magic
        x = x - piece
        pieces.append(piece.astype(BF16))
    return pieces, x


def gram_kernel(a_ref, g_ref, h1, e1, h2, e2, x3, y1, y2, y3):
    k = a_ref.shape[0]
    step = pl.program_id(0)

    @pl.when(step == 0)
    def _():
        for ref in (h1, e1, h2, e2, x3, y1, y2, y3):
            ref[...] = jnp.zeros_like(ref)

    x = a_ref[...]
    scale = power_above(jnp.max(jnp.abs(x), axis=1, keepdims=True))
    pieces, _ = cut(x, scale, (-7, -15, -23))
    stack = jnp.concatenate(pieces, axis=0)
    prod = lax.dot_general(stack, stack, NT, preferred_element_type=F32)
    s, e = two_sum(h1[...], prod[:k, : 2 * k])
    h1[...] = s
    e1[...] += e
    s, e = two_sum(h2[...], prod[k : 2 * k, : 2 * k])
    h2[...] = s
    e2[...] += e
    x3[...] += prod[2 * k :, : 2 * k]
    y1[...] += prod[:k, 2 * k :]
    y2[...] += prod[k : 2 * k, 2 * k :]
    y3[...] += prod[2 * k :, 2 * k :]

    @pl.when(step == pl.num_programs(0) - 1)
    def _():
        a1 = h1[...]
        b1 = e1[...]
        a2 = h2[...]
        left = a1[:, :k]
        d2, f2 = two_sum(a1[:, k:], a2[:, :k])
        low = (a2 + x3[...])[:, k:] + x3[:, :k] + y1[...]
        low = low + (b1[:, :k] + b1[:, k:] + e2[:, :k] + y2[...] + y3[...])
        s, f1 = two_sum(left, d2)
        hi, lo = quick_two_sum(s, f1 + f2 + low)
        g_ref[...] = jnp.concatenate([lo, hi], axis=1)


def local_gram(panel):
    k, n = panel.shape
    wide = pltpu.VMEM((k, 2 * k), F32)
    narrow = pltpu.VMEM((k, k), F32)
    block = 1024
    return pl.pallas_call(
        gram_kernel,
        out_shape=jax.ShapeDtypeStruct((k, 2 * k), F32),
        grid=(n // block,),
        in_specs=[pl.BlockSpec((k, block), lambda i: (0, i))],
        out_specs=pl.BlockSpec((k, 2 * k), lambda i: (0, 0)),
        scratch_shapes=[wide, wide, wide, wide, wide, narrow, narrow, narrow],
    )(panel)


def pair_sum(values, k):
    total, err = values[0], None
    for v in values[1:]:
        total, e = two_sum(total, v)
        err = e if err is None else err + e
    lo = total[:, :k] + err[:, k:]
    hi, lo = quick_two_sum(total[:, k:], lo)
    return jnp.concatenate([lo, hi], axis=1)


def sum_kernel(n_inner, n_grp, p_ref, o_ref, part, slot1, mine, slot2, full, send, recv):
    k = p_ref.shape[0]
    rows = k // n_inner
    ii = lax.axis_index("inner")
    gi = lax.axis_index("grp")
    barrier = pltpu.get_barrier_semaphore()
    for d in range(1, n_inner):
        pl.semaphore_signal(
            barrier, inc=1, device_id={"inner": lax.rem(ii + d, n_inner)},
            device_id_type=pl.DeviceIdType.MESH,
        )
    for d in range(1, n_grp):
        pl.semaphore_signal(
            barrier, inc=1, device_id={"grp": lax.rem(gi + d, n_grp)},
            device_id_type=pl.DeviceIdType.MESH,
        )
    for i in range(n_inner):
        part[i] = p_ref[rows * i : rows * (i + 1), :]
    pl.semaphore_wait(barrier, n_inner + n_grp - 2)

    for d in range(1, n_inner):
        to = lax.rem(ii + d, n_inner)
        pltpu.make_async_remote_copy(
            src_ref=part.at[to], dst_ref=slot1.at[d - 1], send_sem=send.at[0],
            recv_sem=recv.at[0], device_id={"inner": to}, device_id_type=pl.DeviceIdType.MESH,
        ).start()
    pltpu.make_async_copy(slot1, slot1, recv.at[0]).wait()
    mine[0] = pair_sum([part[ii]] + [slot1[d] for d in range(n_inner - 1)], k)

    others = slot2.at[pl.ds(0, n_grp - 1)]
    slot2[gi] = mine[0]
    for d in range(1, n_grp):
        to = lax.rem(gi + d, n_grp)
        pltpu.make_async_remote_copy(
            src_ref=mine.at[0], dst_ref=slot2.at[gi], send_sem=send.at[1],
            recv_sem=recv.at[1], device_id={"grp": to}, device_id_type=pl.DeviceIdType.MESH,
        ).start()
    pltpu.make_async_copy(others, others, recv.at[1]).wait()
    final = pair_sum([slot2[g] for g in range(n_grp)], k)
    full[ii] = final
    mine[1] = final

    for d in range(1, n_inner):
        to = lax.rem(ii + d, n_inner)
        pltpu.make_async_remote_copy(
            src_ref=mine.at[1], dst_ref=full.at[ii], send_sem=send.at[2],
            recv_sem=recv.at[2], device_id={"inner": to}, device_id_type=pl.DeviceIdType.MESH,
        ).start()
    pltpu.make_async_copy(slot1, slot1, recv.at[2]).wait()
    for i in range(n_inner):
        o_ref[rows * i : rows * (i + 1), :] = full[i]
    pltpu.make_async_copy(slot1, slot1, send.at[0]).wait()
    pltpu.make_async_copy(others, others, send.at[1]).wait()
    pltpu.make_async_copy(slot1, slot1, send.at[2]).wait()


def device_sum(pairs):
    k, w = pairs.shape
    n_inner, n_grp = lax.axis_size("inner"), lax.axis_size("grp")
    rows = k // n_inner
    vmem = pl.BlockSpec(memory_space=pltpu.VMEM)
    return pl.pallas_call(
        functools.partial(sum_kernel, n_inner, n_grp),
        out_shape=jax.ShapeDtypeStruct((k, w), F32),
        in_specs=[vmem],
        out_specs=vmem,
        scratch_shapes=[
            pltpu.VMEM((n_inner, rows, w), F32),
            pltpu.VMEM((n_inner - 1, rows, w), F32),
            pltpu.VMEM((2, rows, w), F32),
            pltpu.VMEM((n_grp, rows, w), F32),
            pltpu.VMEM((n_inner, rows, w), F32),
            pltpu.SemaphoreType.DMA((3,)),
            pltpu.SemaphoreType.DMA((3,)),
        ],
        compiler_params=pltpu.CompilerParams(collective_id=0, has_side_effects=True),
    )(pairs)


def eliminate(x, k):
    step = 8
    sub = lax.broadcasted_iota(jnp.int32, (step, 2 * k), 0)
    blocks = k // step
    rows = [x[step * i : step * (i + 1), :] for i in range(blocks)]

    def lanes(v, c):
        return jnp.broadcast_to(v[:, c : c + 1], v.shape)

    def row(v, j):
        return jnp.broadcast_to(v[j : j + 1, :], v.shape)

    for b in range(blocks):
        v = rows[b]
        cols = [[lanes(rows[i], k + step * b + j) for j in range(step)] for i in range(b, blocks)]
        scale = None
        for j in range(step):
            pivot = row(cols[0][j], j)
            inv = 1.0 / pivot
            root = lax.rsqrt(pivot)
            scale = root if scale is None else jnp.where(sub == j, root, scale)
            heads = [row(cols[0][m], j) for m in range(j + 1, step)]
            vj = row(v, j)
            for i in range(b, blocks):
                c = cols[i - b]
                mult = c[j] * inv
                if i == b:
                    mult = jnp.where(sub > j, mult, 0.0)
                    v = v - mult * vj
                else:
                    rows[i] = rows[i] - mult * vj
                for m in range(j + 1, step):
                    c[m] = c[m] - mult * heads[m - j - 1]
        rows[b] = v * scale
    return jnp.concatenate(rows, axis=0)


def factor(g, k, norm):
    r_id = lax.broadcasted_iota(jnp.int32, (k, k), 0)
    c_id = lax.broadcasted_iota(jnp.int32, (k, k), 1)
    eye = r_id == c_id
    lo, hi = g[:, :k], g[:, k:]
    diag = jnp.where(eye, hi, 0.0)

    def unit(d):
        c = lax.rsqrt(d)
        c8 = c * 8388609.0
        return c8 - (c8 - c)

    col = unit(jnp.sum(diag, axis=1, keepdims=True))
    row = unit(jnp.sum(diag, axis=0, keepdims=True))
    hi = hi * col * row
    lo = lo * col * row
    ident = jnp.where(eye, 1.0, 0.0).astype(F32)
    w1 = eliminate(jnp.concatenate([ident, hi], axis=1), k)[:, :k]
    w_pieces, _ = cut(w1, power_above(jnp.max(jnp.abs(w1), axis=1, keepdims=True)), (-7, -15))
    w_stack = jnp.concatenate(w_pieces, axis=0)
    w1 = w_pieces[0].astype(F32) + w_pieces[1].astype(F32)
    top, rest = cut(hi, 4.0, (-7, -15, -23))
    tail, _ = cut(rest + lo, 4.0, (-31, -39, -47))
    g_stack = jnp.concatenate(top + tail, axis=0)
    prod = lax.dot_general(g_stack, w_stack, NT, preferred_element_type=F32)
    s, e = prod[:k, :], 0.0
    for i in range(1, 6):
        s, f = two_sum(s, prod[k * i : k * (i + 1), :])
        e = e + f
    u_hi, f = two_sum(s[:, :k], s[:, k:])
    u_hi, u_lo = quick_two_sum(u_hi, f + e[:, :k] + e[:, k:])
    u_scale = power_above(jnp.max(jnp.abs(u_hi), axis=0, keepdims=True))
    top, rest = cut(u_hi, u_scale, (-7, -15, -23))
    tail, _ = cut(rest + u_lo, u_scale, (-31, -39))
    m_hi, m_lo = None, 0.0
    for piece in top + tail:
        prod = lax.dot_general(w_stack, piece, NN, preferred_element_type=F32)
        for part in (prod[:k, :], prod[k:, :]):
            if m_hi is None:
                m_hi = part
            else:
                m_hi, f = two_sum(m_hi, part)
                m_lo = m_lo + f
    m = m_hi + m_lo
    w2 = eliminate(jnp.concatenate([ident, m], axis=1), k)[:, :k]
    w = lax.dot_general(w2, w1, NN, precision=EXACT, preferred_element_type=F32)
    tri = lax.dot_general(w2, u_hi, NT, precision=EXACT, preferred_element_type=F32)
    w = w * (row * norm)
    tri = jnp.where(c_id >= r_id, tri / (row * norm), 0.0)
    return w, tri


def split3(x):
    a = x.astype(BF16)
    x = x - a.astype(F32)
    b = x.astype(BF16)
    return a, b, (x - b.astype(F32)).astype(BF16)


def apply_kernel(norm, g_ref, a_ref, q_ref, t_ref, w_ref):
    k = g_ref.shape[0]

    @pl.when(pl.program_id(0) == 0)
    def _():
        w, tri = factor(g_ref[...], k, norm)
        t_ref[...] = tri
        w0, w1, w2 = split3(w)
        w_ref[...] = jnp.concatenate([w0, w1, w0, w1, w0, w2], axis=1)

    a0, a1, a2 = split3(a_ref[...])
    stack = jnp.concatenate([a0, a0, a1, a1, a2, a0], axis=0)
    q_ref[...] = lax.dot_general(w_ref[...], stack, NN, preferred_element_type=F32)


def factor_and_apply(g, panel, norm):
    k, n = panel.shape
    block = 2048
    return pl.pallas_call(
        functools.partial(apply_kernel, norm),
        out_shape=(jax.ShapeDtypeStruct((k, n), F32), jax.ShapeDtypeStruct((k, k), F32)),
        grid=(n // block,),
        in_specs=[
            pl.BlockSpec((k, 2 * k), lambda i: (0, 0)),
            pl.BlockSpec((k, block), lambda i: (0, i)),
        ],
        out_specs=(
            pl.BlockSpec((k, block), lambda i: (0, i)),
            pl.BlockSpec((k, k), lambda i: (0, 0)),
        ),
        scratch_shapes=[pltpu.VMEM((k, 6 * k), BF16)],
    )(g, panel)


def per_device(panel):
    n_all = panel.shape[1] * lax.axis_size("inner") * lax.axis_size("grp")
    pairs = local_gram(panel)
    total = device_sum(pairs)
    return factor_and_apply(total, panel, math.sqrt(n_all))


def solution(mesh):
    return jax.shard_map(
        per_device,
        mesh=mesh,
        in_specs=(P(None, ("grp", "inner")),),
        out_specs=(P(None, ("grp", "inner")), P()),
        check_vma=False,
    )
```

```python
import functools
import math

import jax
import jax.numpy as jnp
from jax import lax
from jax.experimental import pallas as pl
from jax.experimental.pallas import tpu as pltpu
from jax.sharding import PartitionSpec as P

F32 = jnp.float32
BF16 = jnp.bfloat16
EXACT = lax.Precision.HIGHEST
NT = (((1,), (1,)), ((), ()))
NN = (((1,), (0,)), ((), ()))


def two_sum(a, b):
    s = a + b
    t = s - a
    return s, (a - (s - t)) + (b - t)


def quick_two_sum(a, b):
    s = a + b
    return s, b - (s - a)


def power_above(m):
    c = m * 8388609.0
    return 2.0 * (c - (c - m))


def cut(x, scale, exponents):
    pieces = []
    for e in exponents:
        magic = scale * (1.5 * 2.0 ** (23 + e))
        piece = (x + magic) - magic
        x = x - piece
        pieces.append(piece.astype(BF16))
    return pieces, x


QUAD = 4
BLOCK = 1024


def local_gram(blocks, k):
    hi = err = low = None
    for x in blocks:
        scale = power_above(jnp.max(jnp.abs(x), axis=1, keepdims=True))
        pieces, _ = cut(x, scale, (-7, -15, -23))
        stack = jnp.concatenate(pieces, axis=0)
        prod = lax.dot_general(stack, stack, NT, preferred_element_type=F32)
        wide = [prod[k * i : k * (i + 1), : 2 * k] for i in range(3)]
        side = [prod[k * i : k * (i + 1), 2 * k :] for i in range(3)]
        if hi is None:
            hi, low = wide[:2], [wide[2], side[0] + side[1] + side[2]]
            err = [jnp.zeros_like(h) for h in hi]
        else:
            for i in range(2):
                hi[i], e = two_sum(hi[i], wide[i])
                err[i] = err[i] + e
            low = [low[0] + wide[2], low[1] + (side[0] + side[1] + side[2])]
    d, f = two_sum(hi[0][:, k:], hi[1][:, :k])
    rest = (hi[1] + low[0] + err[0])[:, k:] + (low[0] + err[0] + err[1])[:, :k] + low[1]
    s, e = two_sum(hi[0][:, :k], d)
    top, rest = quick_two_sum(s, e + f + rest)
    return jnp.concatenate([rest, top], axis=1)


def fold(x, k):
    h = k // 2
    r_id = lax.broadcasted_iota(jnp.int32, (h, 2 * k), 0)
    c_id = lax.rem(lax.broadcasted_iota(jnp.int32, (h, 2 * k), 1), k)
    low = x[h:, :]
    body = jnp.where(c_id >= r_id, x[:h, :], pltpu.roll(low, 2 * k - h, 1))
    diag = jnp.sum(jnp.where(c_id == r_id + h, low, 0.0), axis=0, keepdims=True)
    return body, diag


def unfold(p, k):
    h = k // 2
    r_id = lax.broadcasted_iota(jnp.int32, (h, 2 * k), 0)
    c_id = lax.rem(lax.broadcasted_iota(jnp.int32, (h, 2 * k), 1), k)
    body = p[:h, :]
    top = jnp.where(c_id >= r_id, body, 0.0)
    low = jnp.where(c_id < r_id + h, jnp.where(c_id >= h, pltpu.roll(body, h, 1), 0.0), 0.0)
    low = jnp.where(c_id == r_id + h, p[h : h + 1, :], low)
    full = jnp.concatenate([top, low], axis=0)
    flip = jnp.concatenate([full, jnp.zeros_like(full)], axis=0).T
    off = lax.broadcasted_iota(jnp.int32, (k, k), 0) != lax.broadcasted_iota(jnp.int32, (k, k), 1)
    lo = full[:, :k] + jnp.where(off, flip[:k, :k], 0.0)
    hi = full[:, k:] + jnp.where(off, flip[k:, :k], 0.0)
    return quick_two_sum(hi, lo)


def pair_sum(ref, count, k):
    total, err = two_sum(ref[0], ref[1])
    for i in range(2, count):
        total, e = two_sum(total, ref[i])
        err = err + e
    err = err[..., k:]
    return total + jnp.concatenate([err, jnp.zeros_like(err)], axis=-1)


def sum_kernel(
    n_inner, n_grp, a_ref, o_ref, panel, in_1, grp_1, grp_2, in_2, load, send, recv
):
    k, n = a_ref.shape
    count = n // BLOCK
    ii = lax.axis_index("inner")
    gi = lax.axis_index("grp")
    loads = []
    for b in range(count):
        at = pl.ds(BLOCK * b, BLOCK)
        loads.append(pltpu.make_async_copy(a_ref.at[:, at], panel.at[:, at], load.at[b]))
        loads[-1].start()

    inner = [{"inner": lax.rem(ii + d, n_inner)} for d in range(1, n_inner)]
    grp = [{"grp": lax.rem(gi + d, n_grp)} for d in range(1, n_grp)]
    mesh_id = pl.DeviceIdType.MESH
    barrier = pltpu.get_barrier_semaphore()
    for to in inner + grp:
        pl.semaphore_signal(barrier, inc=1, device_id=to, device_id_type=mesh_id)

    def blocks():
        for b in range(count):
            loads[b].wait()
            yield panel[:, BLOCK * b : BLOCK * (b + 1)]

    body, diag = fold(local_gram(blocks(), k), k)
    n_a, n_b = in_1.shape[1], grp_1.shape[1]
    for q in range(n_b):
        grp_1[gi, q] = body[QUAD * q : QUAD * (q + 1), :]
    for q in range(n_a - 1):
        in_1[ii, q] = body[QUAD * (n_b + q) : QUAD * (n_b + q + 1), :]
    in_1[ii, n_a - 1] = jnp.broadcast_to(diag, (QUAD, 2 * k))
    pl.semaphore_wait(barrier, n_inner + n_grp - 2)

    def share(slots, me, partners, s):
        for to in partners:
            pltpu.make_async_remote_copy(
                src_ref=slots.at[me], dst_ref=slots.at[me], send_sem=send.at[s],
                recv_sem=recv.at[s], device_id=to, device_id_type=mesh_id,
            ).start()

    def drain(slots, partners, sem):
        others = slots.at[pl.ds(0, len(partners))]
        pltpu.make_async_copy(others, others, sem).wait()

    share(in_1, ii, inner, 0)
    share(grp_1, gi, grp, 1)
    drain(in_1, inner, recv.at[0])
    grp_2[gi] = pair_sum(in_1, n_inner, k)
    share(grp_2, gi, grp, 2)
    drain(grp_1, grp, recv.at[1])
    in_2[ii] = pair_sum(grp_1, n_grp, k)
    share(in_2, ii, inner, 3)
    drain(grp_2, grp, recv.at[2])
    last = pair_sum(grp_2, n_grp, k)
    for q in range(n_a):
        o_ref[QUAD * (n_b + q) : QUAD * (n_b + q + 1), :] = last[q]
    drain(in_2, inner, recv.at[3])
    last = pair_sum(in_2, n_inner, k)
    for q in range(n_b):
        o_ref[QUAD * q : QUAD * (q + 1), :] = last[q]
    drain(in_1, inner, send.at[0])
    drain(grp_1, grp, send.at[1])
    drain(grp_2, grp, send.at[2])
    drain(in_2, inner, send.at[3])


def gram_sum(panel):
    k, n = panel.shape
    n_inner, n_grp = lax.axis_size("inner"), lax.axis_size("grp")
    rows = k // 2 + QUAD
    n_b = rows // QUAD // 2
    n_a = rows // QUAD - n_b
    return pl.pallas_call(
        functools.partial(sum_kernel, n_inner, n_grp),
        out_shape=jax.ShapeDtypeStruct((rows, 2 * k), F32),
        in_specs=[pl.BlockSpec(memory_space=pl.ANY)],
        out_specs=pl.BlockSpec(memory_space=pltpu.VMEM),
        scratch_shapes=[
            pltpu.VMEM((k, n), F32),
            pltpu.VMEM((n_inner, n_a, QUAD, 2 * k), F32),
            pltpu.VMEM((n_grp, n_b, QUAD, 2 * k), F32),
            pltpu.VMEM((n_grp, n_a, QUAD, 2 * k), F32),
            pltpu.VMEM((n_inner, n_b, QUAD, 2 * k), F32),
            pltpu.SemaphoreType.DMA((n // BLOCK,)),
            pltpu.SemaphoreType.DMA((4,)),
            pltpu.SemaphoreType.DMA((4,)),
        ],
        compiler_params=pltpu.CompilerParams(
            collective_id=0, has_side_effects=True, vmem_limit_bytes=32 << 20
        ),
    )(panel)


def eliminate(x, k):
    step = 8
    sub = lax.broadcasted_iota(jnp.int32, (step, 2 * k), 0)
    blocks = k // step
    rows = [x[step * i : step * (i + 1), :] for i in range(blocks)]

    def lanes(v, c):
        return jnp.broadcast_to(v[:, c : c + 1], v.shape)

    def row(v, j):
        return jnp.broadcast_to(v[j : j + 1, :], v.shape)

    for b in range(blocks):
        v = rows[b]
        cols = [[lanes(rows[i], k + step * b + j) for j in range(step)] for i in range(b, blocks)]
        scale = None
        for j in range(step):
            pivot = row(cols[0][j], j)
            inv = 1.0 / pivot
            root = lax.rsqrt(pivot)
            scale = root if scale is None else jnp.where(sub == j, root, scale)
            heads = [row(cols[0][m], j) for m in range(j + 1, step)]
            vj = row(v, j)
            for i in range(b, blocks):
                c = cols[i - b]
                mult = c[j] * inv
                if i == b:
                    mult = jnp.where(sub > j, mult, 0.0)
                    v = v - mult * vj
                else:
                    rows[i] = rows[i] - mult * vj
                for m in range(j + 1, step):
                    c[m] = c[m] - mult * heads[m - j - 1]
        rows[b] = v * scale
    return jnp.concatenate(rows, axis=0)


def factor(packed, k, norm):
    r_id = lax.broadcasted_iota(jnp.int32, (k, k), 0)
    c_id = lax.broadcasted_iota(jnp.int32, (k, k), 1)
    eye = r_id == c_id
    hi, lo = unfold(packed, k)
    diag = jnp.where(eye, hi, 0.0)

    def unit(d):
        c = lax.rsqrt(d)
        c8 = c * 8388609.0
        return c8 - (c8 - c)

    col = unit(jnp.sum(diag, axis=1, keepdims=True))
    row = unit(jnp.sum(diag, axis=0, keepdims=True))
    hi = hi * col * row
    lo = lo * col * row
    ident = jnp.where(eye, 1.0, 0.0).astype(F32)
    w1 = eliminate(jnp.concatenate([ident, hi], axis=1), k)[:, :k]
    w_pieces, _ = cut(w1, power_above(jnp.max(jnp.abs(w1), axis=1, keepdims=True)), (-7, -15))
    w_stack = jnp.concatenate(w_pieces, axis=0)
    w1 = w_pieces[0].astype(F32) + w_pieces[1].astype(F32)
    top, rest = cut(hi, 4.0, (-7, -15, -23))
    tail, _ = cut(rest + lo, 4.0, (-31, -39, -47))
    g_stack = jnp.concatenate(top + tail, axis=0)
    prod = lax.dot_general(g_stack, w_stack, NT, preferred_element_type=F32)
    s, e = prod[:k, :], 0.0
    for i in range(1, 6):
        s, f = two_sum(s, prod[k * i : k * (i + 1), :])
        e = e + f
    u_hi, f = two_sum(s[:, :k], s[:, k:])
    u_hi, u_lo = quick_two_sum(u_hi, f + e[:, :k] + e[:, k:])
    u_scale = power_above(jnp.max(jnp.abs(u_hi), axis=0, keepdims=True))
    top, rest = cut(u_hi, u_scale, (-7, -15, -23))
    tail, _ = cut(rest + u_lo, u_scale, (-31, -39))
    m_hi, m_lo = None, 0.0
    for piece in top + tail:
        prod = lax.dot_general(w_stack, piece, NN, preferred_element_type=F32)
        for part in (prod[:k, :], prod[k:, :]):
            if m_hi is None:
                m_hi = part
            else:
                m_hi, f = two_sum(m_hi, part)
                m_lo = m_lo + f
    m = m_hi + m_lo
    w2 = eliminate(jnp.concatenate([ident, m], axis=1), k)[:, :k]
    w = lax.dot_general(w2, w1, NN, precision=EXACT, preferred_element_type=F32)
    tri = lax.dot_general(w2, u_hi, NT, precision=EXACT, preferred_element_type=F32)
    w = w * (row * norm)
    tri = jnp.where(c_id >= r_id, tri / (row * norm), 0.0)
    return w, tri


def split3(x):
    a = x.astype(BF16)
    x = x - a.astype(F32)
    b = x.astype(BF16)
    return a, b, (x - b.astype(F32)).astype(BF16)


def apply_kernel(norm, g_ref, a_ref, q_ref, t_ref, w_ref):
    k = a_ref.shape[0]

    @pl.when(pl.program_id(0) == 0)
    def _():
        w, tri = factor(g_ref[...], k, norm)
        t_ref[...] = tri
        w0, w1, w2 = split3(w)
        w_ref[...] = jnp.concatenate([w0, w1, w0, w1, w0, w2], axis=1)

    a0, a1, a2 = split3(a_ref[...])
    stack = jnp.concatenate([a0, a0, a1, a1, a2, a0], axis=0)
    q_ref[...] = lax.dot_general(w_ref[...], stack, NN, preferred_element_type=F32)


def factor_and_apply(g, panel, norm):
    k, n = panel.shape
    block = 4096
    return pl.pallas_call(
        functools.partial(apply_kernel, norm),
        out_shape=(jax.ShapeDtypeStruct((k, n), F32), jax.ShapeDtypeStruct((k, k), F32)),
        grid=(n // block,),
        in_specs=[
            pl.BlockSpec(g.shape, lambda i: (0, 0)),
            pl.BlockSpec((k, block), lambda i: (0, i)),
        ],
        out_specs=(
            pl.BlockSpec((k, block), lambda i: (0, i)),
            pl.BlockSpec((k, k), lambda i: (0, 0)),
        ),
        scratch_shapes=[pltpu.VMEM((k, 6 * k), BF16)],
        compiler_params=pltpu.CompilerParams(vmem_limit_bytes=32 << 20),
    )(g, panel)


def per_device(panel):
    n_all = panel.shape[1] * lax.axis_size("inner") * lax.axis_size("grp")
    return factor_and_apply(gram_sum(panel), panel, math.sqrt(n_all))


def solution(mesh):
    return jax.shard_map(
        per_device,
        mesh=mesh,
        in_specs=(P(None, ("grp", "inner")),),
        out_specs=(P(None, ("grp", "inner")), P()),
        check_vma=False,
    )
```

```python
import functools
import math

import jax
import jax.numpy as jnp
from jax import lax
from jax.experimental import pallas as pl
from jax.experimental.pallas import tpu as pltpu
from jax.sharding import PartitionSpec as P

F32 = jnp.float32
BF16 = jnp.bfloat16
EXACT = lax.Precision.HIGHEST
NT = (((1,), (1,)), ((), ()))
NN = (((1,), (0,)), ((), ()))


def two_sum(a, b):
    s = a + b
    t = s - a
    return s, (a - (s - t)) + (b - t)


def quick_two_sum(a, b):
    s = a + b
    return s, b - (s - a)


def power_above(m):
    c = m * 8388609.0
    return 2.0 * (c - (c - m))


def cut(x, scale, exponents):
    pieces = []
    for e in exponents:
        magic = scale * (1.5 * 2.0 ** (23 + e))
        piece = (x + magic) - magic
        x = x - piece
        pieces.append(piece.astype(BF16))
    return pieces, x


QUAD = 4
BLOCK = 1024
LOADS = 2
STORES = 4


def add_products(x, sums, k):
    hi_0, hi_1, err_0, err_1, low, side = sums
    scale = power_above(jnp.max(jnp.abs(x), axis=1, keepdims=True))
    pieces, _ = cut(x, scale, (-7, -15, -23))
    stack = jnp.concatenate(pieces, axis=0)
    prod = lax.dot_general(stack, stack, NT, preferred_element_type=F32)
    hi_0, e = two_sum(hi_0, prod[:k, : 2 * k])
    err_0 = err_0 + e
    hi_1, e = two_sum(hi_1, prod[k : 2 * k, : 2 * k])
    err_1 = err_1 + e
    low = low + prod[2 * k :, : 2 * k]
    side = side + (prod[:k, 2 * k :] + prod[k : 2 * k, 2 * k :] + prod[2 * k :, 2 * k :])
    return hi_0, hi_1, err_0, err_1, low, side


def join_products(sums, k):
    hi_0, hi_1, err_0, err_1, low, side = sums
    d, f = two_sum(hi_0[:, k:], hi_1[:, :k])
    rest = (hi_1 + low + err_0)[:, k:] + (low + err_0 + err_1)[:, :k] + side
    s, e = two_sum(hi_0[:, :k], d)
    top, rest = quick_two_sum(s, e + f + rest)
    return jnp.concatenate([rest, top], axis=1)


def fold(x, k):
    h = k // 2
    r_id = lax.broadcasted_iota(jnp.int32, (h, 2 * k), 0)
    c_id = lax.rem(lax.broadcasted_iota(jnp.int32, (h, 2 * k), 1), k)
    low = x[h:, :]
    body = jnp.where(c_id >= r_id, x[:h, :], pltpu.roll(low, 2 * k - h, 1))
    diag = jnp.sum(jnp.where(c_id == r_id + h, low, 0.0), axis=0, keepdims=True)
    return body, diag


def unfold(p, k):
    h = k // 2
    r_id = lax.broadcasted_iota(jnp.int32, (h, 2 * k), 0)
    c_id = lax.rem(lax.broadcasted_iota(jnp.int32, (h, 2 * k), 1), k)
    body = p[:h, :]
    top = jnp.where(c_id >= r_id, body, 0.0)
    low = jnp.where(c_id < r_id + h, jnp.where(c_id >= h, pltpu.roll(body, h, 1), 0.0), 0.0)
    low = jnp.where(c_id == r_id + h, p[h : h + 1, :], low)
    full = jnp.concatenate([top, low], axis=0)
    flip = jnp.concatenate([full, jnp.zeros_like(full)], axis=0).T
    off = lax.broadcasted_iota(jnp.int32, (k, k), 0) != lax.broadcasted_iota(jnp.int32, (k, k), 1)
    lo = full[:, :k] + jnp.where(off, flip[:k, :k], 0.0)
    hi = full[:, k:] + jnp.where(off, flip[k:, :k], 0.0)
    return quick_two_sum(hi, lo)


def pair_sum(ref, count, k):
    total, err = two_sum(ref[0], ref[1])
    for i in range(2, count):
        total, e = two_sum(total, ref[i])
        err = err + e
    err = err[..., k:]
    return total + jnp.concatenate([err, jnp.zeros_like(err)], axis=-1)


def sum_kernel(
    n_inner, n_grp, a_ref, o_ref, panel, in_1, grp_1, grp_2, in_2, load, send, recv
):
    k, n = a_ref.shape
    width = n // LOADS
    ii = lax.axis_index("inner")
    gi = lax.axis_index("grp")

    def arrival(b):
        at = pl.ds(width * b, width)
        return pltpu.make_async_copy(a_ref.at[:, at], panel.at[b], load.at[b])

    for b in range(LOADS):
        arrival(b).start()

    inner = [{"inner": lax.rem(ii + d, n_inner)} for d in range(1, n_inner)]
    grp = [{"grp": lax.rem(gi + d, n_grp)} for d in range(1, n_grp)]
    mesh_id = pl.DeviceIdType.MESH
    barrier = pltpu.get_barrier_semaphore()
    for to in inner + grp:
        pl.semaphore_signal(barrier, inc=1, device_id=to, device_id_type=mesh_id)

    def add_copy(b, sums):
        arrival(b).wait()
        for c in range(width // BLOCK):
            sums = add_products(panel[b, :, BLOCK * c : BLOCK * (c + 1)], sums, k)
        return sums

    zeros = jnp.zeros((k, 2 * k), F32)
    sums = lax.fori_loop(0, LOADS, add_copy, (zeros,) * 5 + (zeros[:, :k],))
    body, diag = fold(join_products(sums, k), k)
    n_a, n_b = in_1.shape[1], grp_1.shape[1]
    for q in range(n_b):
        grp_1[gi, q] = body[QUAD * q : QUAD * (q + 1), :]
    for q in range(n_a - 1):
        in_1[ii, q] = body[QUAD * (n_b + q) : QUAD * (n_b + q + 1), :]
    in_1[ii, n_a - 1] = jnp.broadcast_to(diag, (QUAD, 2 * k))
    pl.semaphore_wait(barrier, n_inner + n_grp - 2)

    def share(slots, me, partners, s):
        for to in partners:
            pltpu.make_async_remote_copy(
                src_ref=slots.at[me], dst_ref=slots.at[me], send_sem=send.at[s],
                recv_sem=recv.at[s], device_id=to, device_id_type=mesh_id,
            ).start()

    def drain(slots, partners, sem):
        others = slots.at[pl.ds(0, len(partners))]
        pltpu.make_async_copy(others, others, sem).wait()

    share(in_1, ii, inner, 0)
    share(grp_1, gi, grp, 1)
    drain(in_1, inner, recv.at[0])
    grp_2[gi] = pair_sum(in_1, n_inner, k)
    share(grp_2, gi, grp, 2)
    drain(grp_1, grp, recv.at[1])
    in_2[ii] = pair_sum(grp_1, n_grp, k)
    share(in_2, ii, inner, 3)
    drain(grp_2, grp, recv.at[2])
    last = pair_sum(grp_2, n_grp, k)
    for q in range(n_a):
        o_ref[QUAD * (n_b + q) : QUAD * (n_b + q + 1), :] = last[q]
    drain(in_2, inner, recv.at[3])
    last = pair_sum(in_2, n_inner, k)
    for q in range(n_b):
        o_ref[QUAD * q : QUAD * (q + 1), :] = last[q]
    drain(in_1, inner, send.at[0])
    drain(grp_1, grp, send.at[1])
    drain(grp_2, grp, send.at[2])
    drain(in_2, inner, send.at[3])


def gram_sum(panel):
    k, n = panel.shape
    n_inner, n_grp = lax.axis_size("inner"), lax.axis_size("grp")
    rows = k // 2 + QUAD
    n_b = rows // QUAD // 2
    n_a = rows // QUAD - n_b
    return pl.pallas_call(
        functools.partial(sum_kernel, n_inner, n_grp),
        out_shape=jax.ShapeDtypeStruct((rows, 2 * k), F32),
        in_specs=[pl.BlockSpec(memory_space=pltpu.HBM)],
        out_specs=pl.BlockSpec(memory_space=pltpu.VMEM),
        scratch_shapes=[
            pltpu.VMEM((LOADS, k, n // LOADS), F32),
            pltpu.VMEM((n_inner, n_a, QUAD, 2 * k), F32),
            pltpu.VMEM((n_grp, n_b, QUAD, 2 * k), F32),
            pltpu.VMEM((n_grp, n_a, QUAD, 2 * k), F32),
            pltpu.VMEM((n_inner, n_b, QUAD, 2 * k), F32),
            pltpu.SemaphoreType.DMA((LOADS,)),
            pltpu.SemaphoreType.DMA((4,)),
            pltpu.SemaphoreType.DMA((4,)),
        ],
        compiler_params=pltpu.CompilerParams(collective_id=0, has_side_effects=True),
    )(panel)


def eliminate(x, k, beside=None):
    step = 8
    sub = lax.broadcasted_iota(jnp.int32, (step, 2 * k), 0)
    blocks = k // step
    rows = [x[step * i : step * (i + 1), :] for i in range(blocks)]

    def lanes(v, c):
        return jnp.broadcast_to(v[:, c : c + 1], v.shape)

    def row(v, j):
        return jnp.broadcast_to(v[j : j + 1, :], v.shape)

    for b in range(blocks):
        v = rows[b]
        cols = [[lanes(rows[i], k + step * b + j) for j in range(step)] for i in range(b, blocks)]
        if beside is not None:
            beside(b)
        top = cols[0]
        diag = None
        for j in range(0, step, 2):
            first, cross = row(top[j], j), row(top[j + 1], j)
            last = row(top[j + 1], j + 1)
            inv_first = 1.0 / first
            inv_last = first * (1.0 / (first * last - cross * cross))
            diag = first if diag is None else jnp.where(sub == j, first, diag)
            diag = jnp.where(sub == j + 1, last - cross * cross * inv_first, diag)
            for p, inv in ((j, inv_first), (j + 1, inv_last)):
                heads = [row(top[m], p) for m in range(p + 1, step)]
                vp = row(v, p)
                for i in range(b, blocks):
                    c = cols[i - b]
                    mult = c[p] * inv
                    if i == b:
                        mult = jnp.where(sub > p, mult, 0.0)
                        v = v - mult * vp
                    else:
                        rows[i] = rows[i] - mult * vp
                    for m in range(p + 1, step):
                        c[m] = c[m] - mult * heads[m - p - 1]
        rows[b] = v * lax.rsqrt(diag)
    return jnp.concatenate(rows, axis=0)


def first_factor(packed, k, w1_ref, g_ref, unit_ref):
    r_id = lax.broadcasted_iota(jnp.int32, (k, k), 0)
    c_id = lax.broadcasted_iota(jnp.int32, (k, k), 1)
    eye = r_id == c_id
    hi, lo = unfold(packed, k)
    diag = jnp.where(eye, hi, 0.0)

    def unit(d):
        c = lax.rsqrt(d)
        c8 = c * 8388609.0
        return c8 - (c8 - c)

    col = unit(jnp.sum(diag, axis=1, keepdims=True))
    row = unit(jnp.sum(diag, axis=0, keepdims=True))
    unit_ref[...] = jnp.broadcast_to(row, unit_ref.shape)
    hi = hi * col * row
    lo = lo * col * row
    top, rest = cut(hi, 4.0, (-7, -15, -23))
    tail, _ = cut(rest + lo, 4.0, (-31, -39, -47))
    for i, piece in enumerate(top + tail):
        g_ref[k * i : k * (i + 1), :] = piece
    ident = jnp.where(eye, 1.0, 0.0).astype(F32)
    w1_ref[...] = eliminate(jnp.concatenate([ident, hi], axis=1), k)[:, :k]


def factor(w1, g_stack, row, k, norm, beside):
    r_id = lax.broadcasted_iota(jnp.int32, (k, k), 0)
    c_id = lax.broadcasted_iota(jnp.int32, (k, k), 1)
    ident = jnp.where(r_id == c_id, 1.0, 0.0).astype(F32)
    w_pieces, _ = cut(w1, power_above(jnp.max(jnp.abs(w1), axis=1, keepdims=True)), (-7, -15))
    w_stack = jnp.concatenate(w_pieces, axis=0)
    w1 = w_pieces[0].astype(F32) + w_pieces[1].astype(F32)
    prod = lax.dot_general(g_stack, w_stack, NT, preferred_element_type=F32)
    s, e = prod[:k, :], 0.0
    for i in range(1, 6):
        s, f = two_sum(s, prod[k * i : k * (i + 1), :])
        e = e + f
    u_hi, f = two_sum(s[:, :k], s[:, k:])
    u_hi, u_lo = quick_two_sum(u_hi, f + e[:, :k] + e[:, k:])
    u_scale = power_above(jnp.max(jnp.abs(u_hi), axis=0, keepdims=True))
    top, rest = cut(u_hi, u_scale, (-7, -15, -23))
    tail, _ = cut(rest + u_lo, u_scale, (-31, -39))
    m_hi, m_lo = None, 0.0
    for piece in top + tail:
        prod = lax.dot_general(w_stack, piece, NN, preferred_element_type=F32)
        for part in (prod[:k, :], prod[k:, :]):
            if m_hi is None:
                m_hi = part
            else:
                m_hi, f = two_sum(m_hi, part)
                m_lo = m_lo + f
    m = m_hi + m_lo
    w2 = eliminate(jnp.concatenate([ident, m], axis=1), k, beside)[:, :k]
    w = lax.dot_general(w2, w1, NN, precision=EXACT, preferred_element_type=F32)
    tri = lax.dot_general(w2, u_hi, NT, precision=EXACT, preferred_element_type=F32)
    w = w * (row * norm)
    tri = jnp.where(c_id >= r_id, tri / (row * norm), 0.0)
    return w, tri


def split3(x):
    a = x.astype(BF16)
    x = x - a.astype(F32)
    b = x.astype(BF16)
    return a, b, (x - b.astype(F32)).astype(BF16)


def apply_kernel(
    norm, p_ref, a_ref, q_ref, t_ref, panel, pieces, out, tri, w1, g_stack, unit, load, store
):
    k, n = a_ref.shape
    width = n // LOADS
    loads = []
    for b in range(LOADS):
        at = pl.ds(width * b, width)
        loads.append(pltpu.make_async_copy(a_ref.at[:, at], panel.at[:, at], load.at[b]))
        loads[-1].start()

    def one_pass(_, carry):
        first_factor(p_ref[...], k, w1, g_stack, unit)
        return carry

    lax.fori_loop(0, jnp.minimum(lax.axis_index("inner") + 1, 1), one_pass, 0)
    for copy in loads:
        copy.wait()

    def split_block(b):
        at = slice(n // 8 * b, n // 8 * (b + 1))
        for i, piece in enumerate(split3(panel[:, at])):
            pieces[k * i : k * (i + 1), at] = piece

    w, tri[...] = factor(w1[...], g_stack[...], unit[:1, :], k, norm, split_block)
    stores = [pltpu.make_async_copy(tri, t_ref, store.at[STORES])]
    stores[0].start()
    w0, w1, w2 = split3(w)
    w = jnp.concatenate([w0, w1, w0, w1, w0, w2], axis=1)
    width = n // STORES
    for b in range(STORES):
        at = pl.ds(width * b, width)
        a0, a1, a2 = (pieces[k * i : k * (i + 1), at] for i in range(3))
        stack = jnp.concatenate([a0, a0, a1, a1, a2, a0], axis=0)
        out[:, at] = lax.dot_general(w, stack, NN, preferred_element_type=F32)
        stores.append(pltpu.make_async_copy(out.at[:, at], q_ref.at[:, at], store.at[b]))
        stores[-1].start()
    for copy in stores:
        copy.wait()


def factor_and_apply(g, panel, norm):
    k, n = panel.shape
    whole = pl.BlockSpec(memory_space=pltpu.VMEM)
    stay = pl.BlockSpec(memory_space=pltpu.HBM)
    return pl.pallas_call(
        functools.partial(apply_kernel, norm),
        out_shape=(jax.ShapeDtypeStruct((k, n), F32), jax.ShapeDtypeStruct((k, k), F32)),
        in_specs=[whole, stay],
        out_specs=(stay, stay),
        scratch_shapes=[
            pltpu.VMEM((k, n), F32),
            pltpu.VMEM((3 * k, n), BF16),
            pltpu.VMEM((k, n), F32),
            pltpu.VMEM((k, k), F32),
            pltpu.VMEM((k, k), F32),
            pltpu.VMEM((6 * k, k), BF16),
            pltpu.VMEM((8, k), F32),
            pltpu.SemaphoreType.DMA((LOADS,)),
            pltpu.SemaphoreType.DMA((STORES + 1,)),
        ],
    )(g, panel)


def per_device(panel):
    n_all = panel.shape[1] * lax.axis_size("inner") * lax.axis_size("grp")
    return factor_and_apply(gram_sum(panel), panel, math.sqrt(n_all))


def solution(mesh):
    return jax.shard_map(
        per_device,
        mesh=mesh,
        in_specs=(P(None, ("grp", "inner")),),
        out_specs=(P(None, ("grp", "inner")), P()),
        check_vma=False,
    )
```

```python
import functools
import math

import jax
import jax.numpy as jnp
from jax import lax
from jax.experimental import pallas as pl
from jax.experimental.pallas import tpu as pltpu
from jax.sharding import PartitionSpec as P

F32 = jnp.float32
BF16 = jnp.bfloat16
EXACT = lax.Precision.HIGHEST
NT = (((1,), (1,)), ((), ()))
NN = (((1,), (0,)), ((), ()))


def two_sum(a, b):
    s = a + b
    t = s - a
    return s, (a - (s - t)) + (b - t)


def quick_two_sum(a, b):
    s = a + b
    return s, b - (s - a)


def power_above(m):
    c = m * 8388609.0
    return 2.0 * (c - (c - m))


def cut(x, scale, exponents):
    pieces = []
    for e in exponents:
        magic = scale * (1.5 * 2.0 ** (23 + e))
        piece = (x + magic) - magic
        x = x - piece
        pieces.append(piece.astype(BF16))
    return pieces, x


QUAD = 4
BLOCK = 1024
LOADS = 2
STORES = 4


def add_products(x, sums, k):
    hi_0, hi_1, err_0, err_1, low, side = sums
    scale = power_above(jnp.max(jnp.abs(x), axis=1, keepdims=True))
    pieces, _ = cut(x, scale, (-7, -15, -23))
    stack = jnp.concatenate(pieces, axis=0)
    prod = lax.dot_general(stack, stack, NT, preferred_element_type=F32)
    hi_0, e = two_sum(hi_0, prod[:k, : 2 * k])
    err_0 = err_0 + e
    hi_1, e = two_sum(hi_1, prod[k : 2 * k, : 2 * k])
    err_1 = err_1 + e
    low = low + prod[2 * k :, : 2 * k]
    side = side + (prod[:k, 2 * k :] + prod[k : 2 * k, 2 * k :] + prod[2 * k :, 2 * k :])
    return hi_0, hi_1, err_0, err_1, low, side


def join_products(sums, k):
    hi_0, hi_1, err_0, err_1, low, side = sums
    d, f = two_sum(hi_0[:, k:], hi_1[:, :k])
    rest = (hi_1 + low + err_0)[:, k:] + (low + err_0 + err_1)[:, :k] + side
    s, e = two_sum(hi_0[:, :k], d)
    top, rest = quick_two_sum(s, e + f + rest)
    return jnp.concatenate([rest, top], axis=1)


def fold(x, k):
    h = k // 2
    r_id = lax.broadcasted_iota(jnp.int32, (h, 2 * k), 0)
    c_id = lax.rem(lax.broadcasted_iota(jnp.int32, (h, 2 * k), 1), k)
    low = x[h:, :]
    body = jnp.where(c_id >= r_id, x[:h, :], pltpu.roll(low, 2 * k - h, 1))
    diag = jnp.sum(jnp.where(c_id == r_id + h, low, 0.0), axis=0, keepdims=True)
    return body, diag


def unfold(p, k):
    h = k // 2
    r_id = lax.broadcasted_iota(jnp.int32, (h, 2 * k), 0)
    c_id = lax.rem(lax.broadcasted_iota(jnp.int32, (h, 2 * k), 1), k)
    body = p[:h, :]
    top = jnp.where(c_id >= r_id, body, 0.0)
    low = jnp.where(c_id < r_id + h, jnp.where(c_id >= h, pltpu.roll(body, h, 1), 0.0), 0.0)
    low = jnp.where(c_id == r_id + h, p[h : h + 1, :], low)
    full = jnp.concatenate([top, low], axis=0)
    flip = jnp.concatenate([full, jnp.zeros_like(full)], axis=0).T
    off = lax.broadcasted_iota(jnp.int32, (k, k), 0) != lax.broadcasted_iota(jnp.int32, (k, k), 1)
    lo = full[:, :k] + jnp.where(off, flip[:k, :k], 0.0)
    hi = full[:, k:] + jnp.where(off, flip[k:, :k], 0.0)
    return quick_two_sum(hi, lo)


def pair_sum(values, k):
    total, err = two_sum(values[0], values[1])
    for v in values[2:]:
        total, e = two_sum(total, v)
        err = err + e
    err = err[..., k:]
    return total + jnp.concatenate([err, jnp.zeros_like(err)], axis=-1)


def far_first(n):
    return sorted(((min(d, n - d), d) for d in range(n)), reverse=True)


def sum_kernel(
    n_inner, n_grp, a_ref, o_ref, panel, halves, half, in_1, col_1, col_2, in_2, load, send, recv
):
    k, n = a_ref.shape
    width = n // LOADS
    ii = lax.axis_index("inner")
    gi = lax.axis_index("grp")

    def arrival(b):
        at = pl.ds(width * b, width)
        return pltpu.make_async_copy(a_ref.at[:, at], panel.at[b], load.at[b])

    for b in range(LOADS):
        arrival(b).start()

    side, depth = math.isqrt(n_inner), n_grp // 2
    y, x = lax.div(ii, side), lax.rem(ii, side)
    level, core = lax.div(gi, 2), lax.rem(gi, 2)
    mate = gi + 1 - 2 * core
    sibling = [(0, {"grp": mate})]
    plane, plane_mates, column, column_mates = [], [], [], []
    for far_y, dy in far_first(side):
        for far_x, dx in far_first(side):
            if dy or dx:
                to = lax.rem(y + dy, side) * side + lax.rem(x + dx, side)
                plane.append((far_y + far_x, {"inner": to}))
                plane_mates.append((far_y + far_x, {"inner": to, "grp": mate}))
    for far, d in far_first(depth):
        if d:
            to = 2 * lax.rem(level + d, depth)
            column.append((far, {"grp": to + core}))
            column_mates.append((far, {"grp": to + 1 - core}))
    mesh_id = pl.DeviceIdType.MESH
    barrier = pltpu.get_barrier_semaphore()
    everyone = plane_mates + column_mates + plane + column + sibling
    for _, to in sorted(everyone, key=lambda p: -p[0]):
        pl.semaphore_signal(barrier, inc=1, device_id=to, device_id_type=mesh_id)

    def add_copy(b, sums):
        arrival(b).wait()
        for c in range(width // BLOCK):
            sums = add_products(panel[b, :, BLOCK * c : BLOCK * (c + 1)], sums, k)
        return sums

    zeros = jnp.zeros((k, 2 * k), F32)
    sums = lax.fori_loop(0, LOADS, add_copy, (zeros,) * 5 + (zeros[:, :k],))
    body, diag = fold(join_products(sums, k), k)
    quads = halves.shape[1]
    n_a, n_b = in_1.shape[1], col_1.shape[1]
    per_body = k // 2 // QUAD
    for q in range(2 * quads):
        if q < per_body:
            piece = body[QUAD * q : QUAD * (q + 1), :]
        else:
            piece = jnp.broadcast_to(diag, (QUAD, 2 * k))
        halves[q // quads, q % quads] = piece
    pl.semaphore_wait(barrier, len(everyone))

    def share(*sets):
        todo = [(far, to, st) for st in sets for far, to in st[2]]
        for _, to, (source, target, _, s) in sorted(todo, key=lambda p: -p[0]):
            pltpu.make_async_remote_copy(
                src_ref=source, dst_ref=target, send_sem=send.at[s],
                recv_sem=recv.at[s], device_id=to, device_id_type=mesh_id,
            ).start()

    def drain(slots, count, sem):
        some = slots.at[pl.ds(0, count)]
        pltpu.make_async_copy(some, some, sem).wait()

    share((halves.at[1 - core], half.at[0], sibling, 0))
    drain(half, 1, recv.at[0])
    mine = pair_sum([halves[core], half[0]], k)
    in_1[ii] = mine[:n_a]
    col_1[level] = mine[n_a:]
    share((in_1.at[ii], in_1.at[ii], plane, 1), (col_1.at[level], col_1.at[level], column, 2))
    drain(in_1, n_inner - 1, recv.at[1])
    col_2[gi] = pair_sum([in_1[i] for i in range(n_inner)], k)
    share((col_2.at[gi], col_2.at[gi], column + column_mates + sibling, 3))
    drain(col_1, depth - 1, recv.at[2])
    place = core * n_inner + ii
    in_2[place] = pair_sum([col_1[i] for i in range(depth)], k)
    share((in_2.at[place], in_2.at[place], plane + plane_mates + sibling, 4))

    def put(value, start):
        for q in range(value.shape[0]):
            if QUAD * (start + q) < o_ref.shape[0]:
                o_ref[QUAD * (start + q) : QUAD * (start + q + 1), :] = value[q]

    drain(col_2, n_grp - 1, recv.at[3])
    for c in range(2):
        put(pair_sum([col_2[2 * i + c] for i in range(depth)], k), quads * c)
    drain(in_2, 2 * n_inner - 1, recv.at[4])
    for c in range(2):
        put(pair_sum([in_2[n_inner * c + i] for i in range(n_inner)], k), quads * c + n_a)
    drain(half, 1, send.at[0])
    drain(in_1, n_inner - 1, send.at[1])
    drain(col_1, depth - 1, send.at[2])
    drain(col_2, n_grp - 1, send.at[3])
    drain(in_2, 2 * n_inner - 1, send.at[4])


def gram_sum(panel):
    k, n = panel.shape
    n_inner, n_grp = lax.axis_size("inner"), lax.axis_size("grp")
    rows = k // 2 + QUAD
    quads = -(-rows // (2 * QUAD))
    n_b = quads // 2
    n_a = quads - n_b

    def slots(count, size):
        return pltpu.VMEM((count, size, QUAD, 2 * k), F32)

    return pl.pallas_call(
        functools.partial(sum_kernel, n_inner, n_grp),
        out_shape=jax.ShapeDtypeStruct((rows, 2 * k), F32),
        in_specs=[pl.BlockSpec(memory_space=pltpu.HBM)],
        out_specs=pl.BlockSpec(memory_space=pltpu.VMEM),
        scratch_shapes=[
            pltpu.VMEM((LOADS, k, n // LOADS), F32),
            slots(2, quads),
            slots(1, quads),
            slots(n_inner, n_a),
            slots(n_grp // 2, n_b),
            slots(n_grp, n_a),
            slots(2 * n_inner, n_b),
            pltpu.SemaphoreType.DMA((LOADS,)),
            pltpu.SemaphoreType.DMA((5,)),
            pltpu.SemaphoreType.DMA((5,)),
        ],
        compiler_params=pltpu.CompilerParams(collective_id=0, has_side_effects=True),
    )(panel)


def eliminate(x, k, beside=None):
    step = 8
    sub = lax.broadcasted_iota(jnp.int32, (step, 2 * k), 0)
    blocks = k // step
    rows = [x[step * i : step * (i + 1), :] for i in range(blocks)]

    def lanes(v, c):
        return jnp.broadcast_to(v[:, c : c + 1], v.shape)

    def row(v, j):
        return jnp.broadcast_to(v[j : j + 1, :], v.shape)

    for b in range(blocks):
        v = rows[b]
        cols = [[lanes(rows[i], k + step * b + j) for j in range(step)] for i in range(b, blocks)]
        if beside is not None:
            beside(b)
        top = cols[0]
        diag = None
        for j in range(0, step, 2):
            first, cross = row(top[j], j), row(top[j + 1], j)
            last = row(top[j + 1], j + 1)
            inv_first = 1.0 / first
            inv_last = first * (1.0 / (first * last - cross * cross))
            diag = first if diag is None else jnp.where(sub == j, first, diag)
            diag = jnp.where(sub == j + 1, last - cross * cross * inv_first, diag)
            for p, inv in ((j, inv_first), (j + 1, inv_last)):
                heads = [row(top[m], p) for m in range(p + 1, step)]
                vp = row(v, p)
                for i in range(b, blocks):
                    c = cols[i - b]
                    mult = c[p] * inv
                    if i == b:
                        mult = jnp.where(sub > p, mult, 0.0)
                        v = v - mult * vp
                    else:
                        rows[i] = rows[i] - mult * vp
                    for m in range(p + 1, step):
                        c[m] = c[m] - mult * heads[m - p - 1]
        rows[b] = v * lax.rsqrt(diag)
    return jnp.concatenate(rows, axis=0)


def first_factor(packed, k, w1_ref, g_ref, unit_ref):
    r_id = lax.broadcasted_iota(jnp.int32, (k, k), 0)
    c_id = lax.broadcasted_iota(jnp.int32, (k, k), 1)
    eye = r_id == c_id
    hi, lo = unfold(packed, k)
    diag = jnp.where(eye, hi, 0.0)

    def unit(d):
        c = lax.rsqrt(d)
        c8 = c * 8388609.0
        return c8 - (c8 - c)

    col = unit(jnp.sum(diag, axis=1, keepdims=True))
    row = unit(jnp.sum(diag, axis=0, keepdims=True))
    unit_ref[...] = jnp.broadcast_to(row, unit_ref.shape)
    hi = hi * col * row
    lo = lo * col * row
    top, rest = cut(hi, 4.0, (-7, -15, -23))
    tail, _ = cut(rest + lo, 4.0, (-31, -39, -47))
    for i, piece in enumerate(top + tail):
        g_ref[k * i : k * (i + 1), :] = piece
    ident = jnp.where(eye, 1.0, 0.0).astype(F32)
    w1_ref[...] = eliminate(jnp.concatenate([ident, hi], axis=1), k)[:, :k]


def factor(w1, g_stack, row, k, norm, beside):
    r_id = lax.broadcasted_iota(jnp.int32, (k, k), 0)
    c_id = lax.broadcasted_iota(jnp.int32, (k, k), 1)
    ident = jnp.where(r_id == c_id, 1.0, 0.0).astype(F32)
    w_pieces, _ = cut(w1, power_above(jnp.max(jnp.abs(w1), axis=1, keepdims=True)), (-7, -15))
    w_stack = jnp.concatenate(w_pieces, axis=0)
    w1 = w_pieces[0].astype(F32) + w_pieces[1].astype(F32)
    prod = lax.dot_general(g_stack, w_stack, NT, preferred_element_type=F32)
    s, e = prod[:k, :], 0.0
    for i in range(1, 6):
        s, f = two_sum(s, prod[k * i : k * (i + 1), :])
        e = e + f
    u_hi, f = two_sum(s[:, :k], s[:, k:])
    u_hi, u_lo = quick_two_sum(u_hi, f + e[:, :k] + e[:, k:])
    u_scale = power_above(jnp.max(jnp.abs(u_hi), axis=0, keepdims=True))
    top, rest = cut(u_hi, u_scale, (-7, -15, -23))
    tail, _ = cut(rest + u_lo, u_scale, (-31, -39))
    m_hi, m_lo = None, 0.0
    for piece in top + tail:
        prod = lax.dot_general(w_stack, piece, NN, preferred_element_type=F32)
        for part in (prod[:k, :], prod[k:, :]):
            if m_hi is None:
                m_hi = part
            else:
                m_hi, f = two_sum(m_hi, part)
                m_lo = m_lo + f
    m = m_hi + m_lo
    w2 = eliminate(jnp.concatenate([ident, m], axis=1), k, beside)[:, :k]
    w = lax.dot_general(w2, w1, NN, precision=EXACT, preferred_element_type=F32)
    tri = lax.dot_general(w2, u_hi, NT, precision=EXACT, preferred_element_type=F32)
    w = w * (row * norm)
    tri = jnp.where(c_id >= r_id, tri / (row * norm), 0.0)
    return w, tri


def split3(x):
    a = x.astype(BF16)
    x = x - a.astype(F32)
    b = x.astype(BF16)
    return a, b, (x - b.astype(F32)).astype(BF16)


def apply_kernel(
    norm, p_ref, a_ref, q_ref, t_ref, panel, pieces, out, tri, w1, g_stack, unit, load, store
):
    k, n = a_ref.shape
    width = n // LOADS
    loads = []
    for b in range(LOADS):
        at = pl.ds(width * b, width)
        loads.append(pltpu.make_async_copy(a_ref.at[:, at], panel.at[:, at], load.at[b]))
        loads[-1].start()

    def one_pass(_, carry):
        first_factor(p_ref[...], k, w1, g_stack, unit)
        return carry

    lax.fori_loop(0, jnp.minimum(lax.axis_index("inner") + 1, 1), one_pass, 0)
    for copy in loads:
        copy.wait()

    def split_block(b):
        at = slice(n // 8 * b, n // 8 * (b + 1))
        for i, piece in enumerate(split3(panel[:, at])):
            pieces[k * i : k * (i + 1), at] = piece

    w, tri[...] = factor(w1[...], g_stack[...], unit[:1, :], k, norm, split_block)
    stores = [pltpu.make_async_copy(tri, t_ref, store.at[STORES])]
    stores[0].start()
    w0, w1, w2 = split3(w)
    w = jnp.concatenate([w0, w1, w0, w1, w0, w2], axis=1)
    width = n // STORES
    for b in range(STORES):
        at = pl.ds(width * b, width)
        a0, a1, a2 = (pieces[k * i : k * (i + 1), at] for i in range(3))
        stack = jnp.concatenate([a0, a0, a1, a1, a2, a0], axis=0)
        out[:, at] = lax.dot_general(w, stack, NN, preferred_element_type=F32)
        stores.append(pltpu.make_async_copy(out.at[:, at], q_ref.at[:, at], store.at[b]))
        stores[-1].start()
    for copy in stores:
        copy.wait()


def factor_and_apply(g, panel, norm):
    k, n = panel.shape
    whole = pl.BlockSpec(memory_space=pltpu.VMEM)
    stay = pl.BlockSpec(memory_space=pltpu.HBM)
    return pl.pallas_call(
        functools.partial(apply_kernel, norm),
        out_shape=(jax.ShapeDtypeStruct((k, n), F32), jax.ShapeDtypeStruct((k, k), F32)),
        in_specs=[whole, stay],
        out_specs=(stay, stay),
        scratch_shapes=[
            pltpu.VMEM((k, n), F32),
            pltpu.VMEM((3 * k, n), BF16),
            pltpu.VMEM((k, n), F32),
            pltpu.VMEM((k, k), F32),
            pltpu.VMEM((k, k), F32),
            pltpu.VMEM((6 * k, k), BF16),
            pltpu.VMEM((8, k), F32),
            pltpu.SemaphoreType.DMA((LOADS,)),
            pltpu.SemaphoreType.DMA((STORES + 1,)),
        ],
    )(g, panel)


def per_device(panel):
    n_all = panel.shape[1] * lax.axis_size("inner") * lax.axis_size("grp")
    return factor_and_apply(gram_sum(panel), panel, math.sqrt(n_all))


def solution(mesh):
    return jax.shard_map(
        per_device,
        mesh=mesh,
        in_specs=(P(None, ("grp", "inner")),),
        out_specs=(P(None, ("grp", "inner")), P()),
        check_vma=False,
    )
```

```python
import functools
import math

import jax
import jax.numpy as jnp
from jax import lax
from jax.experimental import pallas as pl
from jax.experimental.pallas import tpu as pltpu
from jax.sharding import PartitionSpec as P

F32 = jnp.float32
BF16 = jnp.bfloat16
EXACT = lax.Precision.HIGHEST
NT = (((1,), (1,)), ((), ()))
NN = (((1,), (0,)), ((), ()))


def two_sum(a, b):
    s = a + b
    t = s - a
    return s, (a - (s - t)) + (b - t)


def quick_two_sum(a, b):
    s = a + b
    return s, b - (s - a)


def power_above(m):
    c = m * 8388609.0
    return 2.0 * (c - (c - m))


def cut(x, scale, exponents):
    pieces = []
    for e in exponents:
        magic = scale * (1.5 * 2.0 ** (23 + e))
        piece = (x + magic) - magic
        x = x - piece
        pieces.append(piece.astype(BF16))
    return pieces, x


QUAD = 4
BLOCK = 1024
LOADS = 2
STORES = 4


def add_products(x, sums, k):
    hi_0, hi_1, err_0, err_1, low, side = sums
    scale = power_above(jnp.max(jnp.abs(x), axis=1, keepdims=True))
    pieces, _ = cut(x, scale, (-7, -15, -23))
    stack = jnp.concatenate(pieces, axis=0)
    prod = lax.dot_general(stack, stack, NT, preferred_element_type=F32)
    hi_0, e = two_sum(hi_0, prod[:k, : 2 * k])
    err_0 = err_0 + e
    hi_1, e = two_sum(hi_1, prod[k : 2 * k, : 2 * k])
    err_1 = err_1 + e
    low = low + prod[2 * k :, : 2 * k]
    side = side + (prod[:k, 2 * k :] + prod[k : 2 * k, 2 * k :] + prod[2 * k :, 2 * k :])
    return hi_0, hi_1, err_0, err_1, low, side


def join_products(sums, k):
    hi_0, hi_1, err_0, err_1, low, side = sums
    d, f = two_sum(hi_0[:, k:], hi_1[:, :k])
    rest = (hi_1 + low + err_0)[:, k:] + (low + err_0 + err_1)[:, :k] + side
    s, e = two_sum(hi_0[:, :k], d)
    top, rest = quick_two_sum(s, e + f + rest)
    return jnp.concatenate([rest, top], axis=1)


def fold(x, k):
    h = k // 2
    r_id = lax.broadcasted_iota(jnp.int32, (h, 2 * k), 0)
    c_id = lax.rem(lax.broadcasted_iota(jnp.int32, (h, 2 * k), 1), k)
    low = x[h:, :]
    body = jnp.where(c_id >= r_id, x[:h, :], pltpu.roll(low, 2 * k - h, 1))
    diag = jnp.sum(jnp.where(c_id == r_id + h, low, 0.0), axis=0, keepdims=True)
    return body, diag


def unfold(p, k):
    h = k // 2
    r_id = lax.broadcasted_iota(jnp.int32, (h, 2 * k), 0)
    c_id = lax.rem(lax.broadcasted_iota(jnp.int32, (h, 2 * k), 1), k)
    body = p[:h, :]
    top = jnp.where(c_id >= r_id, body, 0.0)
    low = jnp.where(c_id < r_id + h, jnp.where(c_id >= h, pltpu.roll(body, h, 1), 0.0), 0.0)
    low = jnp.where(c_id == r_id + h, p[h : h + 1, :], low)
    full = jnp.concatenate([top, low], axis=0)
    flip = jnp.concatenate([full, jnp.zeros_like(full)], axis=0).T
    off = lax.broadcasted_iota(jnp.int32, (k, k), 0) != lax.broadcasted_iota(jnp.int32, (k, k), 1)
    lo = full[:, :k] + jnp.where(off, flip[:k, :k], 0.0)
    hi = full[:, k:] + jnp.where(off, flip[k:, :k], 0.0)
    return quick_two_sum(hi, lo)


def pair_sum(values, k):
    total, err = two_sum(values[0], values[1])
    for v in values[2:]:
        total, e = two_sum(total, v)
        err = err + e
    err = err[..., k:]
    return total + jnp.concatenate([err, jnp.zeros_like(err)], axis=-1)


def far_first(n):
    return sorted(((min(d, n - d), d) for d in range(n)), reverse=True)


def sum_kernel(
    n_inner, n_grp, a_ref, o_ref, panel, halves, half, in_1, col_1, col_2, in_2, load, send, recv
):
    k, n = a_ref.shape
    width = n // LOADS
    ii = lax.axis_index("inner")
    gi = lax.axis_index("grp")

    def arrival(b):
        at = pl.ds(width * b, width)
        return pltpu.make_async_copy(a_ref.at[:, at], panel.at[b], load.at[b])

    for b in range(LOADS):
        arrival(b).start()

    side, depth = math.isqrt(n_inner), n_grp // 2
    y, x = lax.div(ii, side), lax.rem(ii, side)
    level, core = lax.div(gi, 2), lax.rem(gi, 2)
    mate = gi + 1 - 2 * core
    sibling = [(0, {"grp": mate})]
    plane, plane_mates, column, column_mates = [], [], [], []
    for far_y, dy in far_first(side):
        for far_x, dx in far_first(side):
            if dy or dx:
                to = lax.rem(y + dy, side) * side + lax.rem(x + dx, side)
                plane.append((far_y + far_x, {"inner": to}))
                plane_mates.append((far_y + far_x, {"inner": to, "grp": mate}))
    for far, d in far_first(depth):
        if d:
            to = 2 * lax.rem(level + d, depth)
            column.append((far, {"grp": to + core}))
            column_mates.append((far, {"grp": to + 1 - core}))
    mesh_id = pl.DeviceIdType.MESH
    barrier = pltpu.get_barrier_semaphore()
    everyone = plane_mates + column_mates + plane + column + sibling
    for _, to in sorted(everyone, key=lambda p: -p[0]):
        pl.semaphore_signal(barrier, inc=1, device_id=to, device_id_type=mesh_id)

    def add_copy(b, sums):
        arrival(b).wait()
        for c in range(width // BLOCK):
            sums = add_products(panel[b, :, BLOCK * c : BLOCK * (c + 1)], sums, k)
        return sums

    zeros = jnp.zeros((k, 2 * k), F32)
    sums = lax.fori_loop(0, LOADS, add_copy, (zeros,) * 5 + (zeros[:, :k],))
    body, diag = fold(join_products(sums, k), k)
    quads = halves.shape[1]
    n_a, n_b = in_1.shape[1], col_1.shape[1]
    per_body = k // 2 // QUAD
    for q in range(2 * quads):
        if q < per_body:
            piece = body[QUAD * q : QUAD * (q + 1), :]
        else:
            piece = jnp.broadcast_to(diag, (QUAD, 2 * k))
        halves[q // quads, q % quads] = piece
    pl.semaphore_wait(barrier, len(everyone))

    def share(*sets):
        todo = [(far, to, st) for st in sets for far, to in st[2]]
        for _, to, (source, target, _, s) in sorted(todo, key=lambda p: -p[0]):
            pltpu.make_async_remote_copy(
                src_ref=source, dst_ref=target, send_sem=send.at[s],
                recv_sem=recv.at[s], device_id=to, device_id_type=mesh_id,
            ).start()

    def drain(slots, count, sem):
        some = slots.at[pl.ds(0, count)]
        pltpu.make_async_copy(some, some, sem).wait()

    share((halves.at[1 - core], half.at[0], sibling, 0))
    drain(half, 1, recv.at[0])
    mine = pair_sum([halves[core], half[0]], k)
    in_1[ii] = mine[:n_a]
    col_1[level] = mine[n_a:]
    share((in_1.at[ii], in_1.at[ii], plane, 1), (col_1.at[level], col_1.at[level], column, 2))
    drain(in_1, n_inner - 1, recv.at[1])
    col_2[gi] = pair_sum([in_1[i] for i in range(n_inner)], k)
    share((col_2.at[gi], col_2.at[gi], column + column_mates + sibling, 3))
    drain(col_1, depth - 1, recv.at[2])
    place = core * n_inner + ii
    in_2[place] = pair_sum([col_1[i] for i in range(depth)], k)
    share((in_2.at[place], in_2.at[place], plane + plane_mates + sibling, 4))

    def put(value, start):
        for q in range(value.shape[0]):
            if QUAD * (start + q) < o_ref.shape[0]:
                o_ref[QUAD * (start + q) : QUAD * (start + q + 1), :] = value[q]

    drain(col_2, n_grp - 1, recv.at[3])
    for c in range(2):
        put(pair_sum([col_2[2 * i + c] for i in range(depth)], k), quads * c)
    drain(in_2, 2 * n_inner - 1, recv.at[4])
    for c in range(2):
        put(pair_sum([in_2[n_inner * c + i] for i in range(n_inner)], k), quads * c + n_a)
    drain(half, 1, send.at[0])
    drain(in_1, n_inner - 1, send.at[1])
    drain(col_1, depth - 1, send.at[2])
    drain(col_2, n_grp - 1, send.at[3])
    drain(in_2, 2 * n_inner - 1, send.at[4])


def gram_sum(panel):
    k, n = panel.shape
    n_inner, n_grp = lax.axis_size("inner"), lax.axis_size("grp")
    rows = k // 2 + QUAD
    quads = -(-rows // (2 * QUAD))
    n_b = quads // 2
    n_a = quads - n_b

    def slots(count, size):
        return pltpu.VMEM((count, size, QUAD, 2 * k), F32)

    return pl.pallas_call(
        functools.partial(sum_kernel, n_inner, n_grp),
        out_shape=jax.ShapeDtypeStruct((rows, 2 * k), F32),
        in_specs=[pl.BlockSpec(memory_space=pltpu.HBM)],
        out_specs=pl.BlockSpec(memory_space=pltpu.VMEM),
        scratch_shapes=[
            pltpu.VMEM((LOADS, k, n // LOADS), F32),
            slots(2, quads),
            slots(1, quads),
            slots(n_inner, n_a),
            slots(n_grp // 2, n_b),
            slots(n_grp, n_a),
            slots(2 * n_inner, n_b),
            pltpu.SemaphoreType.DMA((LOADS,)),
            pltpu.SemaphoreType.DMA((5,)),
            pltpu.SemaphoreType.DMA((5,)),
        ],
        compiler_params=pltpu.CompilerParams(collective_id=0, has_side_effects=True),
    )(panel)


def eliminate(x, k):
    step = 8
    sub = lax.broadcasted_iota(jnp.int32, (step, 2 * k), 0)
    blocks = k // step
    rows = [x[step * i : step * (i + 1), :] for i in range(blocks)]

    def lanes(v, c):
        return jnp.broadcast_to(v[:, c : c + 1], v.shape)

    def row(v, j):
        return jnp.broadcast_to(v[j : j + 1, :], v.shape)

    for b in range(blocks):
        v = rows[b]
        cols = [[lanes(rows[i], k + step * b + j) for j in range(step)] for i in range(b, blocks)]
        top = cols[0]
        diag = None
        for j in range(0, step, 2):
            first, cross = row(top[j], j), row(top[j + 1], j)
            last = row(top[j + 1], j + 1)
            inv_first = 1.0 / first
            inv_last = first * (1.0 / (first * last - cross * cross))
            diag = first if diag is None else jnp.where(sub == j, first, diag)
            diag = jnp.where(sub == j + 1, last - cross * cross * inv_first, diag)
            for p, inv in ((j, inv_first), (j + 1, inv_last)):
                heads = [row(top[m], p) for m in range(p + 1, step)]
                vp = row(v, p)
                for i in range(b, blocks):
                    c = cols[i - b]
                    mult = c[p] * inv
                    if i == b:
                        mult = jnp.where(sub > p, mult, 0.0)
                        v = v - mult * vp
                    else:
                        rows[i] = rows[i] - mult * vp
                    for m in range(p + 1, step):
                        c[m] = c[m] - mult * heads[m - p - 1]
        rows[b] = v * lax.rsqrt(diag)
    return jnp.concatenate(rows, axis=0)


def first_factor(packed, k, w1_ref, g_ref, unit_ref):
    r_id = lax.broadcasted_iota(jnp.int32, (k, k), 0)
    c_id = lax.broadcasted_iota(jnp.int32, (k, k), 1)
    eye = r_id == c_id
    hi, lo = unfold(packed, k)
    diag = jnp.where(eye, hi, 0.0)

    def unit(d):
        c = lax.rsqrt(d)
        c8 = c * 8388609.0
        return c8 - (c8 - c)

    col = unit(jnp.sum(diag, axis=1, keepdims=True))
    row = unit(jnp.sum(diag, axis=0, keepdims=True))
    unit_ref[...] = jnp.broadcast_to(row, unit_ref.shape)
    hi = hi * col * row
    lo = lo * col * row
    top, rest = cut(hi, 4.0, (-7, -15, -23))
    tail, _ = cut(rest + lo, 4.0, (-31, -39, -47))
    for i, piece in enumerate(top + tail):
        g_ref[k * i : k * (i + 1), :] = piece
    ident = jnp.where(eye, 1.0, 0.0).astype(F32)
    w1_ref[...] = eliminate(jnp.concatenate([ident, hi], axis=1), k)[:, :k]


def half_lower(x, r_id, c_id):
    return jnp.where(r_id > c_id, x, jnp.where(r_id == c_id, 0.5 * x, 0.0))


def factor(w1, g_stack, row, k, norm, w2_ref, beside):
    r_id = lax.broadcasted_iota(jnp.int32, (k, k), 0)
    c_id = lax.broadcasted_iota(jnp.int32, (k, k), 1)
    ident = jnp.where(r_id == c_id, 1.0, 0.0).astype(F32)
    w_pieces, _ = cut(w1, power_above(jnp.max(jnp.abs(w1), axis=1, keepdims=True)), (-8, -17))
    w_stack = jnp.concatenate(w_pieces, axis=0)
    w1 = w_pieces[0].astype(F32) + w_pieces[1].astype(F32)
    prod = lax.dot_general(g_stack, w_stack, NT, preferred_element_type=F32)
    beside(0, 3)
    part = [prod[k * i : k * (i + 1), :] for i in range(6)]
    s, e = two_sum(part[0], part[1])
    s, f = two_sum(s, part[2])
    e = e + f + (part[3] + (part[4] + part[5]))
    u_hi, f = two_sum(s[:, :k], s[:, k:])
    u_hi, u_lo = quick_two_sum(u_hi, f + e[:, :k] + e[:, k:])
    u_scale = power_above(jnp.max(jnp.abs(u_hi), axis=0, keepdims=True))
    top, rest = cut(u_hi, u_scale, (-7, -15, -23))
    tail, _ = cut(rest + u_lo, u_scale, (-31, -39))
    part = [lax.dot_general(w_stack, p, NN, preferred_element_type=F32) for p in top + tail]
    beside(3, 8)
    large = [part[0][:k], part[0][k:], part[1][:k], part[1][k:], part[2][:k]]
    m_lo = part[2][k:] + part[3][:k] + (part[3][k:] + part[4][:k] + part[4][k:])
    m_hi = large[0]
    for v in large[1:]:
        m_hi, f = two_sum(m_hi, v)
        m_lo = m_lo + f
    rest = (m_hi - ident) + m_lo
    p = half_lower(rest, r_id, c_id)
    p_16 = p.astype(BF16)
    square = lax.dot_general(p_16, p_16, NN, preferred_element_type=F32)
    gram = lax.dot_general(p_16, p_16, NT, preferred_element_type=F32)
    w2_ref[...] = ident - p + (square + half_lower(gram, r_id, c_id))
    small = jnp.sum(p * p) < 2.0**-11

    @pl.when(jnp.logical_not(small))
    def _():
        w2_ref[...] = eliminate(jnp.concatenate([ident, ident + rest], axis=1), k)[:, :k]

    w2 = w2_ref[...]
    w = lax.dot_general(w2, w1, NN, precision=EXACT, preferred_element_type=F32)
    tri = lax.dot_general(w2, u_hi, NT, precision=EXACT, preferred_element_type=F32)
    w = w * (row * norm)
    tri = jnp.where(c_id >= r_id, tri / (row * norm), 0.0)
    return w, tri


def split3(x):
    a = x.astype(BF16)
    x = x - a.astype(F32)
    b = x.astype(BF16)
    return a, b, (x - b.astype(F32)).astype(BF16)


def apply_kernel(
    norm, p_ref, a_ref, q_ref, t_ref, panel, pieces, out, tri, w1, w2, g_stack, unit, load, store
):
    k, n = a_ref.shape
    width = n // LOADS
    loads = []
    for b in range(LOADS):
        at = pl.ds(width * b, width)
        loads.append(pltpu.make_async_copy(a_ref.at[:, at], panel.at[:, at], load.at[b]))
        loads[-1].start()

    def one_pass(_, carry):
        first_factor(p_ref[...], k, w1, g_stack, unit)
        return carry

    lax.fori_loop(0, jnp.minimum(lax.axis_index("inner") + 1, 1), one_pass, 0)
    for copy in loads:
        copy.wait()

    def split_blocks(first, last):
        for b in range(first, last):
            at = slice(n // 8 * b, n // 8 * (b + 1))
            for i, piece in enumerate(split3(panel[:, at])):
                pieces[k * i : k * (i + 1), at] = piece

    w, tri[...] = factor(w1[...], g_stack[...], unit[:1, :], k, norm, w2, split_blocks)
    stores = [pltpu.make_async_copy(tri, t_ref, store.at[STORES])]
    stores[0].start()
    w0, w1, w2 = split3(w)
    w = jnp.concatenate([w0, w1, w0, w1, w0, w2], axis=1)
    width = n // STORES
    for b in range(STORES):
        at = pl.ds(width * b, width)
        a0, a1, a2 = (pieces[k * i : k * (i + 1), at] for i in range(3))
        stack = jnp.concatenate([a0, a0, a1, a1, a2, a0], axis=0)
        out[:, at] = lax.dot_general(w, stack, NN, preferred_element_type=F32)
        stores.append(pltpu.make_async_copy(out.at[:, at], q_ref.at[:, at], store.at[b]))
        stores[-1].start()
    for copy in stores:
        copy.wait()


def factor_and_apply(g, panel, norm):
    k, n = panel.shape
    whole = pl.BlockSpec(memory_space=pltpu.VMEM)
    stay = pl.BlockSpec(memory_space=pltpu.HBM)
    return pl.pallas_call(
        functools.partial(apply_kernel, norm),
        out_shape=(jax.ShapeDtypeStruct((k, n), F32), jax.ShapeDtypeStruct((k, k), F32)),
        in_specs=[whole, stay],
        out_specs=(stay, stay),
        scratch_shapes=[
            pltpu.VMEM((k, n), F32),
            pltpu.VMEM((3 * k, n), BF16),
            pltpu.VMEM((k, n), F32),
            pltpu.VMEM((k, k), F32),
            pltpu.VMEM((k, k), F32),
            pltpu.VMEM((k, k), F32),
            pltpu.VMEM((6 * k, k), BF16),
            pltpu.VMEM((8, k), F32),
            pltpu.SemaphoreType.DMA((LOADS,)),
            pltpu.SemaphoreType.DMA((STORES + 1,)),
        ],
    )(g, panel)


def per_device(panel):
    n_all = panel.shape[1] * lax.axis_size("inner") * lax.axis_size("grp")
    return factor_and_apply(gram_sum(panel), panel, math.sqrt(n_all))


def solution(mesh):
    return jax.shard_map(
        per_device,
        mesh=mesh,
        in_specs=(P(None, ("grp", "inner")),),
        out_specs=(P(None, ("grp", "inner")), P()),
        check_vma=False,
    )
```

```python
import functools
import math

import jax
import jax.numpy as jnp
from jax import lax
from jax.experimental import pallas as pl
from jax.experimental.pallas import tpu as pltpu
from jax.sharding import PartitionSpec as P

F32 = jnp.float32
BF16 = jnp.bfloat16
EXACT = lax.Precision.HIGHEST
NT = (((1,), (1,)), ((), ()))
NN = (((1,), (0,)), ((), ()))


def two_sum(a, b):
    s = a + b
    t = s - a
    return s, (a - (s - t)) + (b - t)


def quick_two_sum(a, b):
    s = a + b
    return s, b - (s - a)


def power_above(m):
    c = m * 8388609.0
    return 2.0 * (c - (c - m))


def cut(x, scale, exponents):
    pieces = []
    for e in exponents:
        magic = scale * (1.5 * 2.0 ** (23 + e))
        piece = (x + magic) - magic
        x = x - piece
        pieces.append(piece.astype(BF16))
    return pieces, x


QUAD = 4
BLOCK = 1024
LOADS = 2
STORES = 8


def add_products(x, sums, k):
    hi_0, hi_1, err_0, err_1, low, side = sums
    scale = power_above(jnp.max(jnp.abs(x), axis=1, keepdims=True))
    pieces, _ = cut(x, scale, (-7, -15, -23))
    stack = jnp.concatenate(pieces, axis=0)
    prod = lax.dot_general(stack, stack, NT, preferred_element_type=F32)
    hi_0, e = two_sum(hi_0, prod[:k, : 2 * k])
    err_0 = err_0 + e
    hi_1, e = two_sum(hi_1, prod[k : 2 * k, : 2 * k])
    err_1 = err_1 + e
    low = low + prod[2 * k :, : 2 * k]
    side = side + (prod[:k, 2 * k :] + prod[k : 2 * k, 2 * k :] + prod[2 * k :, 2 * k :])
    return hi_0, hi_1, err_0, err_1, low, side


def join_products(sums, k):
    hi_0, hi_1, err_0, err_1, low, side = sums
    d, f = two_sum(hi_0[:, k:], hi_1[:, :k])
    rest = (hi_1 + low + err_0)[:, k:] + (low + err_0 + err_1)[:, :k] + side
    s, e = two_sum(hi_0[:, :k], d)
    top, rest = quick_two_sum(s, e + f + rest)
    return jnp.concatenate([rest, top], axis=1)


def fold(x, k):
    h = k // 2
    r_id = lax.broadcasted_iota(jnp.int32, (h, 2 * k), 0)
    c_id = lax.rem(lax.broadcasted_iota(jnp.int32, (h, 2 * k), 1), k)
    low = x[h:, :]
    body = jnp.where(c_id >= r_id, x[:h, :], pltpu.roll(low, 2 * k - h, 1))
    diag = jnp.sum(jnp.where(c_id == r_id + h, low, 0.0), axis=0, keepdims=True)
    return body, diag


def unfold(p, k):
    h = k // 2
    r_id = lax.broadcasted_iota(jnp.int32, (h, 2 * k), 0)
    c_id = lax.rem(lax.broadcasted_iota(jnp.int32, (h, 2 * k), 1), k)
    body = p[:h, :]
    top = jnp.where(c_id >= r_id, body, 0.0)
    low = jnp.where(c_id < r_id + h, jnp.where(c_id >= h, pltpu.roll(body, h, 1), 0.0), 0.0)
    low = jnp.where(c_id == r_id + h, p[h : h + 1, :], low)
    full = jnp.concatenate([top, low], axis=0)
    flip = jnp.concatenate([full, jnp.zeros_like(full)], axis=0).T
    off = lax.broadcasted_iota(jnp.int32, (k, k), 0) != lax.broadcasted_iota(jnp.int32, (k, k), 1)
    lo = full[:, :k] + jnp.where(off, flip[:k, :k], 0.0)
    hi = full[:, k:] + jnp.where(off, flip[k:, :k], 0.0)
    return quick_two_sum(hi, lo)


def pair_sum(values, k):
    total, err = two_sum(values[0], values[1])
    for v in values[2:]:
        total, e = two_sum(total, v)
        err = err + e
    err = err[..., k:]
    return total + jnp.concatenate([err, jnp.zeros_like(err)], axis=-1)


def far_first(n):
    return sorted(((min(d, n - d), d) for d in range(n)), reverse=True)


def sum_kernel(
    n_inner, n_grp, a_ref, o_ref, s_ref, panel, pieces, halves, half, in_1, col_1, col_2, in_2,
    load, send, recv, done
):
    k, n = a_ref.shape
    width = n // LOADS
    ii = lax.axis_index("inner")
    gi = lax.axis_index("grp")

    def arrival(b):
        at = pl.ds(width * b, width)
        return pltpu.make_async_copy(a_ref.at[:, at], panel.at[b], load.at[b])

    for b in range(LOADS):
        arrival(b).start()

    side, depth = math.isqrt(n_inner), n_grp // 2
    y, x = lax.div(ii, side), lax.rem(ii, side)
    level, core = lax.div(gi, 2), lax.rem(gi, 2)
    mate = gi + 1 - 2 * core
    sibling = [(0, {"grp": mate})]
    plane, plane_mates, column, column_mates = [], [], [], []
    for far_y, dy in far_first(side):
        for far_x, dx in far_first(side):
            if dy or dx:
                to = lax.rem(y + dy, side) * side + lax.rem(x + dx, side)
                plane.append((far_y + far_x, {"inner": to}))
                plane_mates.append((far_y + far_x, {"inner": to, "grp": mate}))
    for far, d in far_first(depth):
        if d:
            to = 2 * lax.rem(level + d, depth)
            column.append((far, {"grp": to + core}))
            column_mates.append((far, {"grp": to + 1 - core}))
    mesh_id = pl.DeviceIdType.MESH
    barrier = pltpu.get_barrier_semaphore()
    everyone = plane_mates + column_mates + plane + column + sibling
    for _, to in sorted(everyone, key=lambda p: -p[0]):
        pl.semaphore_signal(barrier, inc=1, device_id=to, device_id_type=mesh_id)

    def add_copy(b, sums):
        arrival(b).wait()
        for c in range(width // BLOCK):
            sums = add_products(panel[b, :, BLOCK * c : BLOCK * (c + 1)], sums, k)
        return sums

    zeros = jnp.zeros((k, 2 * k), F32)
    sums = lax.fori_loop(0, LOADS, add_copy, (zeros,) * 5 + (zeros[:, :k],))
    body, diag = fold(join_products(sums, k), k)
    quads = halves.shape[1]
    n_a, n_b = in_1.shape[1], col_1.shape[1]
    per_body = k // 2 // QUAD
    for q in range(2 * quads):
        if q < per_body:
            piece = body[QUAD * q : QUAD * (q + 1), :]
        else:
            piece = jnp.broadcast_to(diag, (QUAD, 2 * k))
        halves[q // quads, q % quads] = piece
    pl.semaphore_wait(barrier, len(everyone))

    def share(*sets):
        todo = [(far, to, st) for st in sets for far, to in st[2]]
        for _, to, (source, target, _, s) in sorted(todo, key=lambda p: -p[0]):
            pltpu.make_async_remote_copy(
                src_ref=source, dst_ref=target, send_sem=send.at[s],
                recv_sem=recv.at[s], device_id=to, device_id_type=mesh_id,
            ).start()

    def drain(slots, count, sem):
        some = slots.at[pl.ds(0, count)]
        pltpu.make_async_copy(some, some, sem).wait()

    share((halves.at[1 - core], half.at[0], sibling, 0))
    drain(half, 1, recv.at[0])
    mine = pair_sum([halves[core], half[0]], k)
    in_1[ii] = mine[:n_a]
    col_1[level] = mine[n_a:]
    share((in_1.at[ii], in_1.at[ii], plane, 1), (col_1.at[level], col_1.at[level], column, 2))

    def split_panel(_, carry):
        for b in range(LOADS):
            for c in range(0, width, BLOCK):
                for i, piece in enumerate(split3(panel[b, :, c : c + BLOCK])):
                    pieces[k * i : k * (i + 1), width * b + c : width * b + c + BLOCK] = piece
        return carry

    lax.fori_loop(0, jnp.minimum(ii + 1, 1), split_panel, 0)
    keep = pltpu.make_async_copy(pieces, s_ref, done)
    keep.start()
    drain(in_1, n_inner - 1, recv.at[1])
    col_2[gi] = pair_sum([in_1[i] for i in range(n_inner)], k)
    share((col_2.at[gi], col_2.at[gi], column + column_mates + sibling, 3))
    drain(col_1, depth - 1, recv.at[2])
    place = core * n_inner + ii
    in_2[place] = pair_sum([col_1[i] for i in range(depth)], k)
    share((in_2.at[place], in_2.at[place], plane + plane_mates + sibling, 4))

    def put(value, start):
        for q in range(value.shape[0]):
            if QUAD * (start + q) < o_ref.shape[0]:
                o_ref[QUAD * (start + q) : QUAD * (start + q + 1), :] = value[q]

    drain(col_2, n_grp - 1, recv.at[3])
    for c in range(2):
        put(pair_sum([col_2[2 * i + c] for i in range(depth)], k), quads * c)
    drain(in_2, 2 * n_inner - 1, recv.at[4])
    for c in range(2):
        put(pair_sum([in_2[n_inner * c + i] for i in range(n_inner)], k), quads * c + n_a)
    keep.wait()
    drain(half, 1, send.at[0])
    drain(in_1, n_inner - 1, send.at[1])
    drain(col_1, depth - 1, send.at[2])
    drain(col_2, n_grp - 1, send.at[3])
    drain(in_2, 2 * n_inner - 1, send.at[4])


def gram_sum(panel):
    k, n = panel.shape
    n_inner, n_grp = lax.axis_size("inner"), lax.axis_size("grp")
    rows = k // 2 + QUAD
    quads = -(-rows // (2 * QUAD))
    n_b = quads // 2
    n_a = quads - n_b

    def slots(count, size):
        return pltpu.VMEM((count, size, QUAD, 2 * k), F32)

    return pl.pallas_call(
        functools.partial(sum_kernel, n_inner, n_grp),
        out_shape=(
            jax.ShapeDtypeStruct((rows, 2 * k), F32),
            jax.ShapeDtypeStruct((3 * k, n), BF16),
        ),
        in_specs=[pl.BlockSpec(memory_space=pltpu.HBM)],
        out_specs=(
            pl.BlockSpec(memory_space=pltpu.VMEM),
            pl.BlockSpec(memory_space=pltpu.HBM),
        ),
        scratch_shapes=[
            pltpu.VMEM((LOADS, k, n // LOADS), F32),
            pltpu.VMEM((3 * k, n), BF16),
            slots(2, quads),
            slots(1, quads),
            slots(n_inner, n_a),
            slots(n_grp // 2, n_b),
            slots(n_grp, n_a),
            slots(2 * n_inner, n_b),
            pltpu.SemaphoreType.DMA((LOADS,)),
            pltpu.SemaphoreType.DMA((5,)),
            pltpu.SemaphoreType.DMA((5,)),
            pltpu.SemaphoreType.DMA,
        ],
        compiler_params=pltpu.CompilerParams(collective_id=0, has_side_effects=True),
    )(panel)


def eliminate(x, k):
    step = 8
    sub = lax.broadcasted_iota(jnp.int32, (step, 2 * k), 0)
    blocks = k // step
    rows = [x[step * i : step * (i + 1), :] for i in range(blocks)]

    def lanes(v, c):
        return jnp.broadcast_to(v[:, c : c + 1], v.shape)

    def row(v, j):
        return jnp.broadcast_to(v[j : j + 1, :], v.shape)

    for b in range(blocks):
        v = rows[b]
        cols = [[lanes(rows[i], k + step * b + j) for j in range(step)] for i in range(b, blocks)]
        top = cols[0]
        diag = None
        for j in range(0, step, 2):
            first, cross = row(top[j], j), row(top[j + 1], j)
            last = row(top[j + 1], j + 1)
            inv_first = 1.0 / first
            inv_last = first * (1.0 / (first * last - cross * cross))
            diag = first if diag is None else jnp.where(sub == j, first, diag)
            diag = jnp.where(sub == j + 1, last - cross * cross * inv_first, diag)
            for p, inv in ((j, inv_first), (j + 1, inv_last)):
                heads = [row(top[m], p) for m in range(p + 1, step)]
                vp = row(v, p)
                for i in range(b, blocks):
                    c = cols[i - b]
                    mult = c[p] * inv
                    if i == b:
                        mult = jnp.where(sub > p, mult, 0.0)
                        v = v - mult * vp
                    else:
                        rows[i] = rows[i] - mult * vp
                    for m in range(p + 1, step):
                        c[m] = c[m] - mult * heads[m - p - 1]
        rows[b] = v * lax.rsqrt(diag)
    return jnp.concatenate(rows, axis=0)


def first_factor(packed, k):
    r_id = lax.broadcasted_iota(jnp.int32, (k, k), 0)
    c_id = lax.broadcasted_iota(jnp.int32, (k, k), 1)
    eye = r_id == c_id
    hi, lo = unfold(packed, k)
    diag = jnp.where(eye, hi, 0.0)

    def unit(d):
        c = lax.rsqrt(d)
        c8 = c * 8388609.0
        return c8 - (c8 - c)

    col = unit(jnp.sum(diag, axis=1, keepdims=True))
    row = unit(jnp.sum(diag, axis=0, keepdims=True))
    hi = hi * col * row
    lo = lo * col * row
    top, rest = cut(hi, 4.0, (-7, -15, -23))
    tail, _ = cut(rest + lo, 4.0, (-31, -39, -47))
    ident = jnp.where(eye, 1.0, 0.0).astype(F32)
    w1 = eliminate(jnp.concatenate([ident, hi], axis=1), k)[:, :k]
    return w1, jnp.concatenate(top + tail, axis=0), row


def half_lower(x, r_id, c_id):
    return jnp.where(r_id > c_id, x, jnp.where(r_id == c_id, 0.5 * x, 0.0))


def factor(packed, k, norm, w_ref, w2_ref, u_ref, unit_ref):
    w1, g_stack, row = first_factor(packed, k)
    r_id = lax.broadcasted_iota(jnp.int32, (k, k), 0)
    c_id = lax.broadcasted_iota(jnp.int32, (k, k), 1)
    ident = jnp.where(r_id == c_id, 1.0, 0.0).astype(F32)
    w_pieces, _ = cut(w1, power_above(jnp.max(jnp.abs(w1), axis=1, keepdims=True)), (-8, -17))
    w_stack = jnp.concatenate(w_pieces, axis=0)
    w1 = w_pieces[0].astype(F32) + w_pieces[1].astype(F32)
    prod = lax.dot_general(g_stack, w_stack, NT, preferred_element_type=F32)
    part = [prod[k * i : k * (i + 1), :] for i in range(6)]
    s, e = two_sum(part[0], part[1])
    s, f = two_sum(s, part[2])
    e = e + f + (part[3] + (part[4] + part[5]))
    u_hi, f = two_sum(s[:, :k], s[:, k:])
    u_hi, u_lo = quick_two_sum(u_hi, f + e[:, :k] + e[:, k:])
    u_scale = power_above(jnp.max(jnp.abs(u_hi), axis=0, keepdims=True))
    top, rest = cut(u_hi, u_scale, (-7, -15, -23))
    tail, _ = cut(rest + u_lo, u_scale, (-31, -39))
    part = [lax.dot_general(w_stack, p, NN, preferred_element_type=F32) for p in top + tail]
    large = [part[0][:k], part[0][k:], part[1][:k], part[1][k:], part[2][:k]]
    m_lo = part[2][k:] + part[3][:k] + (part[3][k:] + part[4][:k] + part[4][k:])
    m_hi = large[0]
    for v in large[1:]:
        m_hi, f = two_sum(m_hi, v)
        m_lo = m_lo + f
    rest = (m_hi - ident) + m_lo
    p = half_lower(rest, r_id, c_id)
    p_16 = p.astype(BF16)
    square = lax.dot_general(p_16, p_16, NN, preferred_element_type=F32)
    gram = lax.dot_general(p_16, p_16, NT, preferred_element_type=F32)
    w2_ref[...] = ident - p + (square + half_lower(gram, r_id, c_id))
    small = jnp.sum(p * p) < 2.0**-11

    @pl.when(jnp.logical_not(small))
    def _():
        w2_ref[...] = eliminate(jnp.concatenate([ident, ident + rest], axis=1), k)[:, :k]

    w = lax.dot_general(w2_ref[...], w1, NN, precision=EXACT, preferred_element_type=F32)
    w0, w1, w2 = split3(w * (row * norm))
    zero = jnp.zeros_like(w0)
    w_ref[:k, :] = jnp.concatenate([w0, w0, w0], axis=1)
    w_ref[k : 2 * k, :] = jnp.concatenate([w1, w1, zero], axis=1)
    w_ref[2 * k :, :] = jnp.concatenate([w2, zero, zero], axis=1)
    u_ref[...] = u_hi
    unit_ref[...] = jnp.broadcast_to(row * norm, unit_ref.shape)


def split3(x):
    a = x.astype(BF16)
    x = x - a.astype(F32)
    b = x.astype(BF16)
    return a, b, (x - b.astype(F32)).astype(BF16)


def apply_kernel(
    norm, p_ref, s_ref, q_ref, t_ref, pieces, out, tri, w, w2, u, unit, load, store
):
    k, n = q_ref.shape
    arrival = pltpu.make_async_copy(s_ref, pieces, load)
    arrival.start()

    def one_pass(_, carry):
        factor(p_ref[...], k, norm, w, w2, u, unit)
        return carry

    lax.fori_loop(0, jnp.minimum(lax.axis_index("inner") + 1, 1), one_pass, 0)
    arrival.wait()
    stores = []
    width = n // STORES
    for b in range(STORES):
        at = pl.ds(width * b, width)
        prod = lax.dot_general(w[...], pieces[:, at], NN, preferred_element_type=F32)
        out[:, at] = prod[:k] + (prod[k : 2 * k] + prod[2 * k :])
        stores.append(pltpu.make_async_copy(out.at[:, at], q_ref.at[:, at], store.at[b]))
        stores[-1].start()
        if b == 1:
            r = lax.dot_general(w2[...], u[...], NT, precision=EXACT, preferred_element_type=F32)
            r_id = lax.broadcasted_iota(jnp.int32, (k, k), 0)
            c_id = lax.broadcasted_iota(jnp.int32, (k, k), 1)
            tri[...] = jnp.where(c_id >= r_id, r / unit[:1, :], 0.0)
            stores.append(pltpu.make_async_copy(tri, t_ref, store.at[STORES]))
            stores[-1].start()
    for copy in stores:
        copy.wait()


def factor_and_apply(packed, pieces, norm):
    k, n = pieces.shape[0] // 3, pieces.shape[1]
    whole = pl.BlockSpec(memory_space=pltpu.VMEM)
    stay = pl.BlockSpec(memory_space=pltpu.HBM)
    return pl.pallas_call(
        functools.partial(apply_kernel, norm),
        out_shape=(jax.ShapeDtypeStruct((k, n), F32), jax.ShapeDtypeStruct((k, k), F32)),
        in_specs=[whole, stay],
        out_specs=(stay, stay),
        scratch_shapes=[
            pltpu.VMEM((3 * k, n), BF16),
            pltpu.VMEM((k, n), F32),
            pltpu.VMEM((k, k), F32),
            pltpu.VMEM((3 * k, 3 * k), BF16),
            pltpu.VMEM((k, k), F32),
            pltpu.VMEM((k, k), F32),
            pltpu.VMEM((8, k), F32),
            pltpu.SemaphoreType.DMA,
            pltpu.SemaphoreType.DMA((STORES + 1,)),
        ],
    )(packed, pieces)


def per_device(panel):
    n_all = panel.shape[1] * lax.axis_size("inner") * lax.axis_size("grp")
    packed, pieces = gram_sum(panel)
    return factor_and_apply(packed, pieces, math.sqrt(n_all))


def solution(mesh):
    return jax.shard_map(
        per_device,
        mesh=mesh,
        in_specs=(P(None, ("grp", "inner")),),
        out_specs=(P(None, ("grp", "inner")), P()),
        check_vma=False,
    )
```

```python
import functools
import math

import jax
import jax.numpy as jnp
from jax import lax
from jax.experimental import pallas as pl
from jax.experimental.pallas import tpu as pltpu
from jax.sharding import PartitionSpec as P

F32 = jnp.float32
BF16 = jnp.bfloat16
EXACT = lax.Precision.HIGHEST
NT = (((1,), (1,)), ((), ()))
NN = (((1,), (0,)), ((), ()))


def two_sum(a, b):
    s = a + b
    t = s - a
    return s, (a - (s - t)) + (b - t)


def quick_two_sum(a, b):
    s = a + b
    return s, b - (s - a)


def power_above(m):
    c = m * 8388609.0
    return 2.0 * (c - (c - m))


def cut(x, scale, exponents):
    pieces = []
    for e in exponents:
        magic = scale * (1.5 * 2.0 ** (23 + e))
        piece = (x + magic) - magic
        x = x - piece
        pieces.append(piece.astype(BF16))
    return pieces, x


QUAD = 4
BLOCK = 1024
LOADS = 2
STORES = 8


def add_products(x, sums, k):
    hi_0, hi_1, err_0, err_1, low, side = sums
    scale = power_above(jnp.max(jnp.abs(x), axis=1, keepdims=True))
    pieces, _ = cut(x, scale, (-7, -15, -23))
    stack = jnp.concatenate(pieces, axis=0)
    prod = lax.dot_general(stack, stack, NT, preferred_element_type=F32)
    hi_0, e = two_sum(hi_0, prod[:k, : 2 * k])
    err_0 = err_0 + e
    hi_1, e = two_sum(hi_1, prod[k : 2 * k, : 2 * k])
    err_1 = err_1 + e
    low = low + prod[2 * k :, : 2 * k]
    side = side + (prod[:k, 2 * k :] + prod[k : 2 * k, 2 * k :] + prod[2 * k :, 2 * k :])
    return hi_0, hi_1, err_0, err_1, low, side


def join_products(sums, k):
    hi_0, hi_1, err_0, err_1, low, side = sums
    d, f = two_sum(hi_0[:, k:], hi_1[:, :k])
    rest = (hi_1 + low + err_0)[:, k:] + (low + err_0 + err_1)[:, :k] + side
    s, e = two_sum(hi_0[:, :k], d)
    top, rest = quick_two_sum(s, e + f + rest)
    return jnp.concatenate([rest, top], axis=1)


def fold(x, k):
    h = k // 2
    r_id = lax.broadcasted_iota(jnp.int32, (h, 2 * k), 0)
    c_id = lax.rem(lax.broadcasted_iota(jnp.int32, (h, 2 * k), 1), k)
    low = x[h:, :]
    body = jnp.where(c_id >= r_id, x[:h, :], pltpu.roll(low, 2 * k - h, 1))
    diag = jnp.sum(jnp.where(c_id == r_id + h, low, 0.0), axis=0, keepdims=True)
    return body, diag


def unfold(p, k):
    h = k // 2
    r_id = lax.broadcasted_iota(jnp.int32, (h, 2 * k), 0)
    c_id = lax.rem(lax.broadcasted_iota(jnp.int32, (h, 2 * k), 1), k)
    body = p[:h, :]
    top = jnp.where(c_id >= r_id, body, 0.0)
    low = jnp.where(c_id < r_id + h, jnp.where(c_id >= h, pltpu.roll(body, h, 1), 0.0), 0.0)
    low = jnp.where(c_id == r_id + h, p[h : h + 1, :], low)
    full = jnp.concatenate([top, low], axis=0)
    flip = jnp.concatenate([full, jnp.zeros_like(full)], axis=0).T
    off = lax.broadcasted_iota(jnp.int32, (k, k), 0) != lax.broadcasted_iota(jnp.int32, (k, k), 1)
    lo = full[:, :k] + jnp.where(off, flip[:k, :k], 0.0)
    hi = full[:, k:] + jnp.where(off, flip[k:, :k], 0.0)
    return quick_two_sum(hi, lo)


def pair_sum(values, k):
    total, err = two_sum(values[0], values[1])
    for v in values[2:]:
        total, e = two_sum(total, v)
        err = err + e
    err = err[..., k:]
    return total + jnp.concatenate([err, jnp.zeros_like(err)], axis=-1)


def far_first(n):
    return sorted(((min(d, n - d), d) for d in range(n)), reverse=True)


def sum_kernel(
    n_inner, n_grp, a_ref, o_ref, s_ref, panel, pieces, halves, half, in_1, col_1, col_2, in_2,
    load, send, recv, done
):
    k, n = a_ref.shape
    width = n // LOADS
    ii = lax.axis_index("inner")
    gi = lax.axis_index("grp")

    def arrival(b):
        at = pl.ds(width * b, width)
        return pltpu.make_async_copy(a_ref.at[:, at], panel.at[b], load.at[b])

    for b in range(LOADS):
        arrival(b).start()

    side, depth = math.isqrt(n_inner), n_grp // 2
    y, x = lax.div(ii, side), lax.rem(ii, side)
    level, core = lax.div(gi, 2), lax.rem(gi, 2)
    mate = gi + 1 - 2 * core
    sibling = [(0, {"grp": mate})]
    plane, plane_mates, column, column_mates = [], [], [], []
    for far_y, dy in far_first(side):
        for far_x, dx in far_first(side):
            if dy or dx:
                to = lax.rem(y + dy, side) * side + lax.rem(x + dx, side)
                plane.append((far_y + far_x, {"inner": to}))
                plane_mates.append((far_y + far_x, {"inner": to, "grp": mate}))
    for far, d in far_first(depth):
        if d:
            to = 2 * lax.rem(level + d, depth)
            column.append((far, {"grp": to + core}))
            column_mates.append((far, {"grp": to + 1 - core}))
    mesh_id = pl.DeviceIdType.MESH
    barrier = pltpu.get_barrier_semaphore()
    everyone = plane_mates + column_mates + plane + column + sibling
    for _, to in sorted(everyone, key=lambda p: -p[0]):
        pl.semaphore_signal(barrier, inc=1, device_id=to, device_id_type=mesh_id)

    def add_copy(b, sums):
        arrival(b).wait()
        for c in range(width // BLOCK):
            sums = add_products(panel[b, :, BLOCK * c : BLOCK * (c + 1)], sums, k)
        return sums

    zeros = jnp.zeros((k, 2 * k), F32)
    sums = lax.fori_loop(0, LOADS, add_copy, (zeros,) * 5 + (zeros[:, :k],))
    body, diag = fold(join_products(sums, k), k)
    quads = halves.shape[1]
    n_a, n_b = in_1.shape[1], col_1.shape[1]
    per_body = k // 2 // QUAD
    for q in range(2 * quads):
        if q < per_body:
            piece = body[QUAD * q : QUAD * (q + 1), :]
        else:
            piece = jnp.broadcast_to(diag, (QUAD, 2 * k))
        halves[q // quads, q % quads] = piece
    pl.semaphore_wait(barrier, len(everyone))

    def share(*sets):
        todo = [(far, to, st) for st in sets for far, to in st[2]]
        for _, to, (source, target, _, s) in sorted(todo, key=lambda p: -p[0]):
            pltpu.make_async_remote_copy(
                src_ref=source, dst_ref=target, send_sem=send.at[s],
                recv_sem=recv.at[s], device_id=to, device_id_type=mesh_id,
            ).start()

    def drain(slots, count, sem):
        some = slots.at[pl.ds(0, count)]
        pltpu.make_async_copy(some, some, sem).wait()

    share((halves.at[1 - core], half.at[0], sibling, 0))
    drain(half, 1, recv.at[0])
    mine = pair_sum([halves[core], half[0]], k)
    in_1[ii] = mine[:n_a]
    col_1[level] = mine[n_a:]
    share((in_1.at[ii], in_1.at[ii], plane, 1), (col_1.at[level], col_1.at[level], column, 2))

    def split_panel(_, carry):
        for b in range(LOADS):
            for c in range(0, width, BLOCK):
                for i, piece in enumerate(split3(panel[b, :, c : c + BLOCK])):
                    pieces[k * i : k * (i + 1), width * b + c : width * b + c + BLOCK] = piece
        return carry

    lax.fori_loop(0, jnp.minimum(ii + 1, 1), split_panel, 0)
    keep = pltpu.make_async_copy(pieces, s_ref, done)
    keep.start()
    drain(in_1, n_inner - 1, recv.at[1])
    col_2[gi] = pair_sum([in_1[i] for i in range(n_inner)], k)
    share((col_2.at[gi], col_2.at[gi], column + column_mates + sibling, 3))
    drain(col_1, depth - 1, recv.at[2])
    place = core * n_inner + ii
    in_2[place] = pair_sum([col_1[i] for i in range(depth)], k)
    share((in_2.at[place], in_2.at[place], plane + plane_mates + sibling, 4))

    def put(value, start):
        for q in range(value.shape[0]):
            if QUAD * (start + q) < o_ref.shape[0]:
                o_ref[QUAD * (start + q) : QUAD * (start + q + 1), :] = value[q]

    drain(col_2, n_grp - 1, recv.at[3])
    for c in range(2):
        put(pair_sum([col_2[2 * i + c] for i in range(depth)], k), quads * c)
    drain(in_2, 2 * n_inner - 1, recv.at[4])
    for c in range(2):
        put(pair_sum([in_2[n_inner * c + i] for i in range(n_inner)], k), quads * c + n_a)
    keep.wait()
    drain(half, 1, send.at[0])
    drain(in_1, n_inner - 1, send.at[1])
    drain(col_1, depth - 1, send.at[2])
    drain(col_2, n_grp - 1, send.at[3])
    drain(in_2, 2 * n_inner - 1, send.at[4])


def gram_sum(panel):
    k, n = panel.shape
    n_inner, n_grp = lax.axis_size("inner"), lax.axis_size("grp")
    rows = k // 2 + QUAD
    quads = -(-rows // (2 * QUAD))
    n_b = quads // 2
    n_a = quads - n_b

    def slots(count, size):
        return pltpu.VMEM((count, size, QUAD, 2 * k), F32)

    return pl.pallas_call(
        functools.partial(sum_kernel, n_inner, n_grp),
        out_shape=(
            jax.ShapeDtypeStruct((rows, 2 * k), F32),
            jax.ShapeDtypeStruct((3 * k, n), BF16),
        ),
        in_specs=[pl.BlockSpec(memory_space=pltpu.HBM)],
        out_specs=(
            pl.BlockSpec(memory_space=pltpu.VMEM),
            pl.BlockSpec(memory_space=pltpu.HBM),
        ),
        scratch_shapes=[
            pltpu.VMEM((LOADS, k, n // LOADS), F32),
            pltpu.VMEM((3 * k, n), BF16),
            slots(2, quads),
            slots(1, quads),
            slots(n_inner, n_a),
            slots(n_grp // 2, n_b),
            slots(n_grp, n_a),
            slots(2 * n_inner, n_b),
            pltpu.SemaphoreType.DMA((LOADS,)),
            pltpu.SemaphoreType.DMA((5,)),
            pltpu.SemaphoreType.DMA((5,)),
            pltpu.SemaphoreType.DMA,
        ],
        compiler_params=pltpu.CompilerParams(collective_id=0, has_side_effects=True),
    )(panel)


def eliminate(x, k):
    step = 8
    sub = lax.broadcasted_iota(jnp.int32, (step, 2 * k), 0)
    blocks = k // step
    rows = [x[step * i : step * (i + 1), :] for i in range(blocks)]

    def lanes(v, c):
        return jnp.broadcast_to(v[:, c : c + 1], v.shape)

    def row(v, j):
        return jnp.broadcast_to(v[j : j + 1, :], v.shape)

    for b in range(blocks):
        v = rows[b]
        cols = [[lanes(rows[i], k + step * b + j) for j in range(step)] for i in range(b, blocks)]
        top = cols[0]
        diag = None
        for j in range(0, step, 2):
            first, cross = row(top[j], j), row(top[j + 1], j)
            last = row(top[j + 1], j + 1)
            inv_first = 1.0 / first
            inv_last = first * (1.0 / (first * last - cross * cross))
            diag = first if diag is None else jnp.where(sub == j, first, diag)
            diag = jnp.where(sub == j + 1, last - cross * cross * inv_first, diag)
            for p, inv in ((j, inv_first), (j + 1, inv_last)):
                heads = [row(top[m], p) for m in range(p + 1, step)]
                vp = row(v, p)
                for i in range(b, blocks):
                    c = cols[i - b]
                    mult = c[p] * inv
                    if i == b:
                        mult = jnp.where(sub > p, mult, 0.0)
                        v = v - mult * vp
                    else:
                        rows[i] = rows[i] - mult * vp
                    for m in range(p + 1, step):
                        c[m] = c[m] - mult * heads[m - p - 1]
        rows[b] = v * lax.rsqrt(diag)
    return jnp.concatenate(rows, axis=0)


def first_factor(packed, k):
    r_id = lax.broadcasted_iota(jnp.int32, (k, k), 0)
    c_id = lax.broadcasted_iota(jnp.int32, (k, k), 1)
    eye = r_id == c_id
    hi, lo = unfold(packed, k)
    diag = jnp.where(eye, hi, 0.0)

    def unit(d):
        c = lax.rsqrt(d)
        c8 = c * 8388609.0
        return c8 - (c8 - c)

    col = unit(jnp.sum(diag, axis=1, keepdims=True))
    row = unit(jnp.sum(diag, axis=0, keepdims=True))
    hi = hi * col * row
    lo = lo * col * row
    top, rest = cut(hi, 4.0, (-7, -15, -23))
    tail, _ = cut(rest + lo, 4.0, (-31, -39, -47))
    ident = jnp.where(eye, 1.0, 0.0).astype(F32)
    w1 = eliminate(jnp.concatenate([ident, hi], axis=1), k)[:, :k]
    return w1, jnp.concatenate(top + tail, axis=0), row


def half_lower(x, r_id, c_id):
    return jnp.where(r_id > c_id, x, jnp.where(r_id == c_id, 0.5 * x, 0.0))


def factor(packed, k, norm, w_ref, w2_ref, u_ref, unit_ref):
    w1, g_stack, row = first_factor(packed, k)
    r_id = lax.broadcasted_iota(jnp.int32, (k, k), 0)
    c_id = lax.broadcasted_iota(jnp.int32, (k, k), 1)
    ident = jnp.where(r_id == c_id, 1.0, 0.0).astype(F32)
    w_pieces, _ = cut(w1, power_above(jnp.max(jnp.abs(w1), axis=1, keepdims=True)), (-8, -17))
    w_stack = jnp.concatenate(w_pieces, axis=0)
    w1 = w_pieces[0].astype(F32) + w_pieces[1].astype(F32)
    prod = lax.dot_general(g_stack, w_stack, NT, preferred_element_type=F32)
    part = [prod[k * i : k * (i + 1), :] for i in range(6)]
    s, e = two_sum(part[0], part[1])
    s, f = two_sum(s, part[2])
    e = e + f + (part[3] + (part[4] + part[5]))
    u_hi, f = two_sum(s[:, :k], s[:, k:])
    u_hi, u_lo = quick_two_sum(u_hi, f + e[:, :k] + e[:, k:])
    u_scale = power_above(jnp.max(jnp.abs(u_hi), axis=0, keepdims=True))
    top, rest = cut(u_hi, u_scale, (-7, -15, -23))
    tail, _ = cut(rest + u_lo, u_scale, (-31, -39))
    part = [lax.dot_general(w_stack, p, NN, preferred_element_type=F32) for p in top + tail]
    large = [part[0][:k], part[0][k:], part[1][:k], part[1][k:], part[2][:k]]
    m_lo = part[2][k:] + part[3][:k] + (part[3][k:] + part[4][:k] + part[4][k:])
    m_hi = large[0]
    for v in large[1:]:
        m_hi, f = two_sum(m_hi, v)
        m_lo = m_lo + f
    rest = (m_hi - ident) + m_lo
    p = half_lower(rest, r_id, c_id)
    p_16 = p.astype(BF16)
    square = lax.dot_general(p_16, p_16, NN, preferred_element_type=F32)
    gram = lax.dot_general(p_16, p_16, NT, preferred_element_type=F32)
    small = jnp.sum(p * p) < 2.0**-11

    def finish(w2):
        w2_ref[...] = w2
        w = lax.dot_general(w2, w1, NN, precision=EXACT, preferred_element_type=F32)
        pieces = split3(w * (row * norm))
        zero = jnp.zeros_like(pieces[0])
        for i in range(3):
            line = [pieces[i]] * (3 - i) + [zero] * i
            w_ref[k * i : k * (i + 1), :] = jnp.concatenate(line, axis=1)

    finish(ident - p + (square + half_lower(gram, r_id, c_id)))

    @pl.when(jnp.logical_not(small))
    def _():
        finish(eliminate(jnp.concatenate([ident, ident + rest], axis=1), k)[:, :k])

    u_ref[...] = u_hi
    unit_ref[...] = jnp.broadcast_to(row * norm, unit_ref.shape)


def split3(x):
    a = x.astype(BF16)
    x = x - a.astype(F32)
    b = x.astype(BF16)
    return a, b, (x - b.astype(F32)).astype(BF16)


def apply_kernel(
    norm, p_ref, s_ref, q_ref, t_ref, pieces, out, tri, w, w2, u, unit, load, store
):
    k, n = q_ref.shape
    arrival = pltpu.make_async_copy(s_ref, pieces, load)
    arrival.start()

    def one_pass(_, carry):
        factor(p_ref[...], k, norm, w, w2, u, unit)
        return carry

    lax.fori_loop(0, jnp.minimum(lax.axis_index("inner") + 1, 1), one_pass, 0)
    arrival.wait()
    stores = []
    width = n // STORES
    for b in range(STORES):
        at = pl.ds(width * b, width)
        prod = lax.dot_general(w[...], pieces[:, at], NN, preferred_element_type=F32)
        out[:, at] = prod[:k] + (prod[k : 2 * k] + prod[2 * k :])
        stores.append(pltpu.make_async_copy(out.at[:, at], q_ref.at[:, at], store.at[b]))
        stores[-1].start()
        if b == 1:
            r = lax.dot_general(w2[...], u[...], NT, precision=EXACT, preferred_element_type=F32)
            r_id = lax.broadcasted_iota(jnp.int32, (k, k), 0)
            c_id = lax.broadcasted_iota(jnp.int32, (k, k), 1)
            tri[...] = jnp.where(c_id >= r_id, r / unit[:1, :], 0.0)
            stores.append(pltpu.make_async_copy(tri, t_ref, store.at[STORES]))
            stores[-1].start()
    for copy in stores:
        copy.wait()


def factor_and_apply(packed, pieces, norm):
    k, n = pieces.shape[0] // 3, pieces.shape[1]
    whole = pl.BlockSpec(memory_space=pltpu.VMEM)
    stay = pl.BlockSpec(memory_space=pltpu.HBM)
    return pl.pallas_call(
        functools.partial(apply_kernel, norm),
        out_shape=(jax.ShapeDtypeStruct((k, n), F32), jax.ShapeDtypeStruct((k, k), F32)),
        in_specs=[whole, stay],
        out_specs=(stay, stay),
        scratch_shapes=[
            pltpu.VMEM((3 * k, n), BF16),
            pltpu.VMEM((k, n), F32),
            pltpu.VMEM((k, k), F32),
            pltpu.VMEM((3 * k, 3 * k), BF16),
            pltpu.VMEM((k, k), F32),
            pltpu.VMEM((k, k), F32),
            pltpu.VMEM((8, k), F32),
            pltpu.SemaphoreType.DMA,
            pltpu.SemaphoreType.DMA((STORES + 1,)),
        ],
    )(packed, pieces)


def per_device(panel):
    n_all = panel.shape[1] * lax.axis_size("inner") * lax.axis_size("grp")
    packed, pieces = gram_sum(panel)
    return factor_and_apply(packed, pieces, math.sqrt(n_all))


def solution(mesh):
    return jax.shard_map(
        per_device,
        mesh=mesh,
        in_specs=(P(None, ("grp", "inner")),),
        out_specs=(P(None, ("grp", "inner")), P()),
        check_vma=False,
    )
```

```python
import functools
import math

import jax
import jax.numpy as jnp
from jax import lax
from jax.experimental import pallas as pl
from jax.experimental.pallas import tpu as pltpu
from jax.sharding import PartitionSpec as P

F32 = jnp.float32
BF16 = jnp.bfloat16
EXACT = lax.Precision.HIGHEST
NT = (((1,), (1,)), ((), ()))
NN = (((1,), (0,)), ((), ()))


def two_sum(a, b):
    s = a + b
    t = s - a
    return s, (a - (s - t)) + (b - t)


def quick_two_sum(a, b):
    s = a + b
    return s, b - (s - a)


def power_above(m):
    c = m * 8388609.0
    return 2.0 * (c - (c - m))


def cut(x, scale, exponents):
    pieces = []
    for e in exponents:
        magic = scale * (1.5 * 2.0 ** (23 + e))
        piece = (x + magic) - magic
        x = x - piece
        pieces.append(piece.astype(BF16))
    return pieces, x


QUAD = 4
BLOCK = 1024
STORES = 8


def add_products(x, sums, k):
    hi_0, hi_1, err_0, err_1, low, side = sums
    scale = power_above(jnp.max(jnp.abs(x), axis=1, keepdims=True))
    pieces, _ = cut(x, scale, (-7, -15, -23))
    stack = jnp.concatenate(pieces, axis=0)
    prod = lax.dot_general(stack, stack, NT, preferred_element_type=F32)
    hi_0, e = two_sum(hi_0, prod[:k, : 2 * k])
    err_0 = err_0 + e
    hi_1, e = two_sum(hi_1, prod[k : 2 * k, : 2 * k])
    err_1 = err_1 + e
    low = low + prod[2 * k :, : 2 * k]
    side = side + (prod[:k, 2 * k :] + prod[k : 2 * k, 2 * k :] + prod[2 * k :, 2 * k :])
    return hi_0, hi_1, err_0, err_1, low, side


def join_products(sums, k):
    hi_0, hi_1, err_0, err_1, low, side = sums
    d, f = two_sum(hi_0[:, k:], hi_1[:, :k])
    rest = (hi_1 + low + err_0)[:, k:] + (low + err_0 + err_1)[:, :k] + side
    s, e = two_sum(hi_0[:, :k], d)
    top, rest = quick_two_sum(s, e + f + rest)
    return jnp.concatenate([rest, top], axis=1)


def fold(x, k):
    h = k // 2
    r_id = lax.broadcasted_iota(jnp.int32, (h, 2 * k), 0)
    c_id = lax.rem(lax.broadcasted_iota(jnp.int32, (h, 2 * k), 1), k)
    low = x[h:, :]
    body = jnp.where(c_id >= r_id, x[:h, :], pltpu.roll(low, 2 * k - h, 1))
    diag = jnp.sum(jnp.where(c_id == r_id + h, low, 0.0), axis=0, keepdims=True)
    return body, diag


def unfold(p, k):
    h = k // 2
    r_id = lax.broadcasted_iota(jnp.int32, (h, 2 * k), 0)
    c_id = lax.rem(lax.broadcasted_iota(jnp.int32, (h, 2 * k), 1), k)
    body = p[:h, :]
    top = jnp.where(c_id >= r_id, body, 0.0)
    low = jnp.where(c_id < r_id + h, jnp.where(c_id >= h, pltpu.roll(body, h, 1), 0.0), 0.0)
    low = jnp.where(c_id == r_id + h, p[h : h + 1, :], low)
    full = jnp.concatenate([top, low], axis=0)
    flip = jnp.concatenate([full, jnp.zeros_like(full)], axis=0).T
    off = lax.broadcasted_iota(jnp.int32, (k, k), 0) != lax.broadcasted_iota(jnp.int32, (k, k), 1)
    lo = full[:, :k] + jnp.where(off, flip[:k, :k], 0.0)
    hi = full[:, k:] + jnp.where(off, flip[k:, :k], 0.0)
    return quick_two_sum(hi, lo)


def pair_sum(values, k):
    total, err = two_sum(values[0], values[1])
    for v in values[2:]:
        total, e = two_sum(total, v)
        err = err + e
    err = err[..., k:]
    return total + jnp.concatenate([err, jnp.zeros_like(err)], axis=-1)


def far_first(n):
    return sorted(((min(d, n - d), d) for d in range(n)), reverse=True)


def sum_kernel(
    n_inner, n_grp, a_ref, o_ref, s_ref, panel, pieces, halves, half, in_1, col_1, col_2, in_2,
    load, send, recv, done
):
    k, n = a_ref.shape
    ii = lax.axis_index("inner")
    gi = lax.axis_index("grp")

    edges = (0, (n // BLOCK * 3 // 8) * BLOCK, n)
    loads = []
    for b in range(2):
        at = pl.ds(edges[b], edges[b + 1] - edges[b])
        loads.append(pltpu.make_async_copy(a_ref.at[:, at], panel.at[:, at], load.at[b]))
        loads[-1].start()

    side, depth = math.isqrt(n_inner), n_grp // 2
    y, x = lax.div(ii, side), lax.rem(ii, side)
    level, core = lax.div(gi, 2), lax.rem(gi, 2)
    mate = gi + 1 - 2 * core
    sibling = [(0, {"grp": mate})]
    plane, plane_mates, column, column_mates = [], [], [], []
    for far_y, dy in far_first(side):
        for far_x, dx in far_first(side):
            if dy or dx:
                to = lax.rem(y + dy, side) * side + lax.rem(x + dx, side)
                plane.append((far_y + far_x, {"inner": to}))
                plane_mates.append((far_y + far_x, {"inner": to, "grp": mate}))
    for far, d in far_first(depth):
        if d:
            to = 2 * lax.rem(level + d, depth)
            column.append((far, {"grp": to + core}))
            column_mates.append((far, {"grp": to + 1 - core}))
    mesh_id = pl.DeviceIdType.MESH
    barrier = pltpu.get_barrier_semaphore()
    everyone = plane_mates + column_mates + plane + column + sibling
    for _, to in sorted(everyone, key=lambda p: -p[0]):
        pl.semaphore_signal(barrier, inc=1, device_id=to, device_id_type=mesh_id)

    def add_copy(b):
        def add(_, sums):
            loads[b].wait()
            for c in range(edges[b], edges[b + 1], BLOCK):
                sums = add_products(panel[:, c : c + BLOCK], sums, k)
            return sums

        return add

    one = jnp.minimum(ii + 1, 1)
    zeros = jnp.zeros((k, 2 * k), F32)
    sums = (zeros,) * 5 + (zeros[:, :k],)
    for b in range(2):
        sums = lax.fori_loop(0, one, add_copy(b), sums)
    body, diag = fold(join_products(sums, k), k)
    quads = halves.shape[1]
    n_a, n_b = in_1.shape[1], col_1.shape[1]
    per_body = k // 2 // QUAD
    for q in range(2 * quads):
        if q < per_body:
            piece = body[QUAD * q : QUAD * (q + 1), :]
        else:
            piece = jnp.broadcast_to(diag, (QUAD, 2 * k))
        halves[q // quads, q % quads] = piece
    pl.semaphore_wait(barrier, len(everyone))

    def share(*sets):
        todo = [(far, to, st) for st in sets for far, to in st[2]]
        for _, to, (source, target, _, s) in sorted(todo, key=lambda p: -p[0]):
            pltpu.make_async_remote_copy(
                src_ref=source, dst_ref=target, send_sem=send.at[s],
                recv_sem=recv.at[s], device_id=to, device_id_type=mesh_id,
            ).start()

    def drain(slots, count, sem):
        some = slots.at[pl.ds(0, count)]
        pltpu.make_async_copy(some, some, sem).wait()

    share((halves.at[1 - core], half.at[0], sibling, 0))
    drain(half, 1, recv.at[0])
    mine = pair_sum([halves[core], half[0]], k)
    in_1[ii] = mine[:n_a]
    col_1[level] = mine[n_a:]
    share((in_1.at[ii], in_1.at[ii], plane, 1), (col_1.at[level], col_1.at[level], column, 2))

    def split_panel(_, carry):
        for c in range(0, n, BLOCK):
            for i, piece in enumerate(split3(panel[:, c : c + BLOCK])):
                pieces[k * i : k * (i + 1), c : c + BLOCK] = piece
        return carry

    lax.fori_loop(0, one, split_panel, 0)
    keep = pltpu.make_async_copy(pieces, s_ref, done)
    keep.start()
    drain(in_1, n_inner - 1, recv.at[1])
    col_2[gi] = pair_sum([in_1[i] for i in range(n_inner)], k)
    share((col_2.at[gi], col_2.at[gi], column + column_mates + sibling, 3))
    drain(col_1, depth - 1, recv.at[2])
    place = core * n_inner + ii
    in_2[place] = pair_sum([col_1[i] for i in range(depth)], k)
    share((in_2.at[place], in_2.at[place], plane + plane_mates + sibling, 4))

    def put(value, start):
        for q in range(value.shape[0]):
            if QUAD * (start + q) < o_ref.shape[0]:
                o_ref[QUAD * (start + q) : QUAD * (start + q + 1), :] = value[q]

    drain(col_2, n_grp - 1, recv.at[3])
    for c in range(2):
        put(pair_sum([col_2[2 * i + c] for i in range(depth)], k), quads * c)
    drain(in_2, 2 * n_inner - 1, recv.at[4])
    for c in range(2):
        put(pair_sum([in_2[n_inner * c + i] for i in range(n_inner)], k), quads * c + n_a)
    keep.wait()
    drain(half, 1, send.at[0])
    drain(in_1, n_inner - 1, send.at[1])
    drain(col_1, depth - 1, send.at[2])
    drain(col_2, n_grp - 1, send.at[3])
    drain(in_2, 2 * n_inner - 1, send.at[4])


def gram_sum(panel):
    k, n = panel.shape
    n_inner, n_grp = lax.axis_size("inner"), lax.axis_size("grp")
    rows = k // 2 + QUAD
    quads = -(-rows // (2 * QUAD))
    n_b = quads // 2
    n_a = quads - n_b

    def slots(count, size):
        return pltpu.VMEM((count, size, QUAD, 2 * k), F32)

    return pl.pallas_call(
        functools.partial(sum_kernel, n_inner, n_grp),
        out_shape=(
            jax.ShapeDtypeStruct((rows, 2 * k), F32),
            jax.ShapeDtypeStruct((3 * k, n), BF16),
        ),
        in_specs=[pl.BlockSpec(memory_space=pltpu.HBM)],
        out_specs=(
            pl.BlockSpec(memory_space=pltpu.VMEM),
            pl.BlockSpec(memory_space=pltpu.HBM),
        ),
        scratch_shapes=[
            pltpu.VMEM((k, n), F32),
            pltpu.VMEM((3 * k, n), BF16),
            slots(2, quads),
            slots(1, quads),
            slots(n_inner, n_a),
            slots(n_grp // 2, n_b),
            slots(n_grp, n_a),
            slots(2 * n_inner, n_b),
            pltpu.SemaphoreType.DMA((2,)),
            pltpu.SemaphoreType.DMA((5,)),
            pltpu.SemaphoreType.DMA((5,)),
            pltpu.SemaphoreType.DMA,
        ],
        compiler_params=pltpu.CompilerParams(collective_id=0, has_side_effects=True),
    )(panel)


def eliminate(x, k):
    step = 8
    sub = lax.broadcasted_iota(jnp.int32, (step, 2 * k), 0)
    blocks = k // step
    rows = [x[step * i : step * (i + 1), :] for i in range(blocks)]

    def lanes(v, c):
        return jnp.broadcast_to(v[:, c : c + 1], v.shape)

    def row(v, j):
        return jnp.broadcast_to(v[j : j + 1, :], v.shape)

    for b in range(blocks):
        v = rows[b]
        cols = [[lanes(rows[i], k + step * b + j) for j in range(step)] for i in range(b, blocks)]
        top = cols[0]
        diag = None
        for j in range(0, step, 2):
            first, cross = row(top[j], j), row(top[j + 1], j)
            last = row(top[j + 1], j + 1)
            inv_first = 1.0 / first
            inv_last = first * (1.0 / (first * last - cross * cross))
            diag = first if diag is None else jnp.where(sub == j, first, diag)
            diag = jnp.where(sub == j + 1, last - cross * cross * inv_first, diag)
            for p, inv in ((j, inv_first), (j + 1, inv_last)):
                heads = [row(top[m], p) for m in range(p + 1, step)]
                vp = row(v, p)
                for i in range(b, blocks):
                    c = cols[i - b]
                    mult = c[p] * inv
                    if i == b:
                        mult = jnp.where(sub > p, mult, 0.0)
                        v = v - mult * vp
                    else:
                        rows[i] = rows[i] - mult * vp
                    for m in range(p + 1, step):
                        c[m] = c[m] - mult * heads[m - p - 1]
        rows[b] = v * lax.rsqrt(diag)
    return jnp.concatenate(rows, axis=0)


def first_factor(packed, k):
    r_id = lax.broadcasted_iota(jnp.int32, (k, k), 0)
    c_id = lax.broadcasted_iota(jnp.int32, (k, k), 1)
    eye = r_id == c_id
    hi, lo = unfold(packed, k)
    diag = jnp.where(eye, hi, 0.0)

    def unit(d):
        c = lax.rsqrt(d)
        c8 = c * 8388609.0
        return c8 - (c8 - c)

    col = unit(jnp.sum(diag, axis=1, keepdims=True))
    row = unit(jnp.sum(diag, axis=0, keepdims=True))
    hi = hi * col * row
    lo = lo * col * row
    top, rest = cut(hi, 4.0, (-7, -15, -23))
    tail, _ = cut(rest + lo, 4.0, (-31, -39, -47))
    ident = jnp.where(eye, 1.0, 0.0).astype(F32)
    w1 = eliminate(jnp.concatenate([ident, hi], axis=1), k)[:, :k]
    return w1, jnp.concatenate(top + tail, axis=0), row


def half_lower(x, r_id, c_id):
    return jnp.where(r_id > c_id, x, jnp.where(r_id == c_id, 0.5 * x, 0.0))


def factor(packed, k, norm, w_ref, w2_ref, u_ref, unit_ref):
    w1, g_stack, row = first_factor(packed, k)
    r_id = lax.broadcasted_iota(jnp.int32, (k, k), 0)
    c_id = lax.broadcasted_iota(jnp.int32, (k, k), 1)
    ident = jnp.where(r_id == c_id, 1.0, 0.0).astype(F32)
    w_pieces, _ = cut(w1, power_above(jnp.max(jnp.abs(w1), axis=1, keepdims=True)), (-8, -17))
    w_stack = jnp.concatenate(w_pieces, axis=0)
    w1 = w_pieces[0].astype(F32) + w_pieces[1].astype(F32)
    prod = lax.dot_general(g_stack, w_stack, NT, preferred_element_type=F32)
    part = [prod[k * i : k * (i + 1), :] for i in range(6)]
    s, e = two_sum(part[0], part[1])
    s, f = two_sum(s, part[2])
    e = e + f + (part[3] + (part[4] + part[5]))
    u_hi, f = two_sum(s[:, :k], s[:, k:])
    u_hi, u_lo = quick_two_sum(u_hi, f + e[:, :k] + e[:, k:])
    u_scale = power_above(jnp.max(jnp.abs(u_hi), axis=0, keepdims=True))
    top, rest = cut(u_hi, u_scale, (-7, -15, -23))
    tail, _ = cut(rest + u_lo, u_scale, (-31, -39))
    part = [lax.dot_general(w_stack, p, NN, preferred_element_type=F32) for p in top + tail]
    large = [part[0][:k], part[0][k:], part[1][:k], part[1][k:], part[2][:k]]
    m_lo = part[2][k:] + part[3][:k] + (part[3][k:] + part[4][:k] + part[4][k:])
    m_hi = large[0]
    for v in large[1:]:
        m_hi, f = two_sum(m_hi, v)
        m_lo = m_lo + f
    rest = (m_hi - ident) + m_lo
    p = half_lower(rest, r_id, c_id)
    p_16 = p.astype(BF16)
    square = lax.dot_general(p_16, p_16, NN, preferred_element_type=F32)
    gram = lax.dot_general(p_16, p_16, NT, preferred_element_type=F32)
    small = jnp.sum(p * p) < 2.0**-11

    def finish(w2):
        w2_ref[...] = w2
        w = lax.dot_general(w2, w1, NN, precision=EXACT, preferred_element_type=F32)
        pieces = split3(w * (row * norm))
        zero = jnp.zeros_like(pieces[0])
        for i in range(3):
            line = [pieces[i]] * (3 - i) + [zero] * i
            w_ref[k * i : k * (i + 1), :] = jnp.concatenate(line, axis=1)

    finish(ident - p + (square + half_lower(gram, r_id, c_id)))

    @pl.when(jnp.logical_not(small))
    def _():
        finish(eliminate(jnp.concatenate([ident, ident + rest], axis=1), k)[:, :k])

    u_ref[...] = u_hi
    unit_ref[...] = jnp.broadcast_to(row * norm, unit_ref.shape)


def split3(x):
    a = x.astype(BF16)
    x = x - a.astype(F32)
    b = x.astype(BF16)
    return a, b, (x - b.astype(F32)).astype(BF16)


def apply_kernel(
    norm, p_ref, s_ref, q_ref, t_ref, pieces, out, tri, w, w2, u, unit, load, store
):
    k, n = q_ref.shape
    arrival = pltpu.make_async_copy(s_ref, pieces, load)
    arrival.start()

    def one_pass(_, carry):
        factor(p_ref[...], k, norm, w, w2, u, unit)
        return carry

    lax.fori_loop(0, jnp.minimum(lax.axis_index("inner") + 1, 1), one_pass, 0)
    arrival.wait()
    stores = []
    width = n // STORES
    for b in range(STORES):
        at = pl.ds(width * b, width)
        prod = lax.dot_general(w[...], pieces[:, at], NN, preferred_element_type=F32)
        out[:, at] = prod[:k] + (prod[k : 2 * k] + prod[2 * k :])
        stores.append(pltpu.make_async_copy(out.at[:, at], q_ref.at[:, at], store.at[b]))
        stores[-1].start()
        if b == 1:
            r = lax.dot_general(w2[...], u[...], NT, precision=EXACT, preferred_element_type=F32)
            r_id = lax.broadcasted_iota(jnp.int32, (k, k), 0)
            c_id = lax.broadcasted_iota(jnp.int32, (k, k), 1)
            tri[...] = jnp.where(c_id >= r_id, r / unit[:1, :], 0.0)
            stores.append(pltpu.make_async_copy(tri, t_ref, store.at[STORES]))
            stores[-1].start()
    for copy in stores:
        copy.wait()


def factor_and_apply(packed, pieces, norm):
    k, n = pieces.shape[0] // 3, pieces.shape[1]
    whole = pl.BlockSpec(memory_space=pltpu.VMEM)
    stay = pl.BlockSpec(memory_space=pltpu.HBM)
    return pl.pallas_call(
        functools.partial(apply_kernel, norm),
        out_shape=(jax.ShapeDtypeStruct((k, n), F32), jax.ShapeDtypeStruct((k, k), F32)),
        in_specs=[whole, stay],
        out_specs=(stay, stay),
        scratch_shapes=[
            pltpu.VMEM((3 * k, n), BF16),
            pltpu.VMEM((k, n), F32),
            pltpu.VMEM((k, k), F32),
            pltpu.VMEM((3 * k, 3 * k), BF16),
            pltpu.VMEM((k, k), F32),
            pltpu.VMEM((k, k), F32),
            pltpu.VMEM((8, k), F32),
            pltpu.SemaphoreType.DMA,
            pltpu.SemaphoreType.DMA((STORES + 1,)),
        ],
    )(packed, pieces)


def per_device(panel):
    n_all = panel.shape[1] * lax.axis_size("inner") * lax.axis_size("grp")
    packed, pieces = gram_sum(panel)
    return factor_and_apply(packed, pieces, math.sqrt(n_all))


def solution(mesh):
    return jax.shard_map(
        per_device,
        mesh=mesh,
        in_specs=(P(None, ("grp", "inner")),),
        out_specs=(P(None, ("grp", "inner")), P()),
        check_vma=False,
    )
```
